512 devices in a mesh: seq: 128 (over z, x, y_hi), hap: 4 (over y_lo, core).
Axes of the slice: x: 4, y: 8 (y_hi: 4, y_lo: 2; y = y_hi * 2 + y_lo), z: 8, core: 2. Of those that a mesh axis runs over, the one named last changes fastest.
Arguments:
- tokens: bfloat16 [4, 16384, 512], P('hap', 'seq'), may hold values from -24 to 24
- cotangent: bfloat16 [4, 16384, 512], P('hap', 'seq'), may hold values from -6 to 6
- gaps: int32 [128, 2], P('seq'), may hold values from 0 to 128, as said below
- conv_taps: float32 [2, 3, 512], replicated, may hold values from -3.5 to 3.5
- norm_gains: float32 [2, 512], replicated, may hold values from 0.25 to 1.75
- projection: bfloat16 [2, 512, 1024], replicated, may hold values from -0.25 to 0.25
Outputs:
- tokens_grad: bfloat16 [4, 16384, 512], P('hap', 'seq')
- projection_grad: float32 [2, 512, 1024], P(None, 'seq')
- taps_grad: float32 [2, 3, 512], replicated
- gains_grad: float32 [2, 512], replicated
The draws below stay inside these ranges and needn't reach their ends.
Inputs may be any that keep to these rules, and one draw needn't show every extreme that they name: `gaps`: each row holds a start and an end with start <= end; some run is wholly a gap and some has none; gap density varies from region to region.
All inputs are finite; a program needn't handle non-finite values.
Results may differ from the reference program's by a relative error of at most 0.0058.
Values may be sent and summed in bfloat16 or wider, within the bound.
No kernel may reach another device: no remote copies, remote signals or barrier semaphores. Data moves between devices by JAX's collectives and lax.ppermute only.
A program may use at most 64 MiB of HBM per device.

```python
import jax
import jax.numpy as jnp
from jax import lax

C = 512
PROJ = 1024
DILATION_BINS = 32
LAYERS = 2
BINS = 16384
HAPS = 4
BLOCKS = 128


def draw_gaps(key, part):
    key = jax.random.fold_in(key, 7)
    key_rate, key_take, key_length, key_start = jax.random.split(key, 4)
    region_rate = jax.random.randint(key_rate, (BLOCKS // 4,), 0, 4)
    block_rate = jnp.repeat(region_rate, 4)
    chosen = jax.random.randint(key_take, (BLOCKS,), 0, 4) < block_rate
    length = jnp.where(chosen, jax.random.randint(key_length, (BLOCKS,), 1, 129), 0)
    length = length.at[0].set(0).at[1].set(0).at[BLOCKS - 1].set(128)
    start = jax.random.randint(key_start, (BLOCKS,), 0, 129 - length)
    return jnp.stack([start, start + length], 1).astype(jnp.int32)


def spiked(values, rng, source, target, parts, factor):
    owner, partner = [(jnp.arange(values.shape[axis_at]) // (values.shape[axis_at] // parts)).reshape([-1 if axis == axis_at else 1 for axis in range(values.ndim)]) for axis_at in (source, target)]
    chosen = jax.random.permutation(rng, parts)[partner]
    strong = (owner == chosen) | (owner == (partner + parts // 2) % parts)
    return jnp.where(strong, factor * values, values)


def steps_of(own_key, shape, pieces, low, top_value):
    factor_of, own = 1.0, jax.random.fold_in(own_key, 6)
    for axis_at, shards_of in pieces:
        heights = jnp.exp(jax.random.uniform(jax.random.fold_in(own, axis_at), (shards_of,), jnp.float32, low / len(pieces), top_value / len(pieces)))
        factor_of = factor_of * jnp.repeat(heights, shape[axis_at] // shards_of).reshape([-1 if axis == axis_at else 1 for axis in range(len(shape))])
    return factor_of


def bell_draw(stream_key, extent, width, most, cuts=(), held_as=jnp.bfloat16):
    result = width * jax.random.normal(stream_key, extent, jnp.float32)
    if cuts:
        result = result * steps_of(stream_key, extent, cuts, -0.22, 0.18)
    return jnp.clip(result, -most, most).astype(held_as)


def noise_with(rng, dims, width, bound, shards, heavy, kind=jnp.bfloat16):
    drawn = width * jax.random.normal(rng, dims, jnp.float32)
    if shards:
        drawn = drawn * steps_of(rng, dims, shards, -0.22, 0.18)
    return jnp.clip(spiked(drawn, jax.random.fold_in(rng, 3), *heavy), -bound, bound).astype(kind)


def setup_inputs(seed: int = 0) -> dict:
    splits = jax.random.split(jax.random.key(seed), 7)
    tokens = noise_with(splits[0], (HAPS, BINS, C), 1.0, 24.0, ((0, 4), (1, 128)), (1, 2, 128, 5.5))
    cotangent = bell_draw(splits[1], (HAPS, BINS, C), 1.0, 6.0, ((0, 4), (1, 128)))
    gaps = draw_gaps(jax.random.fold_in(splits[6], 71), 0)
    conv_taps = bell_draw(splits[3], (LAYERS, 3, C), 3 ** -0.5, 3.5, (), jnp.float32)
    norm_gains = jnp.clip(1.0 + 0.15 * jax.random.normal(splits[4], (LAYERS, C), jnp.float32), 0.25, 1.75)
    projection = bell_draw(splits[5], (LAYERS, C, PROJ), C ** -0.5, 0.25)
    return {"tokens": tokens, "cotangent": cotangent, "gaps": gaps, "conv_taps": conv_taps, "norm_gains": norm_gains, "projection": projection}


EPS = 1e-06

def valid_of(gap_rows):
    offsets = jnp.arange(128, dtype=jnp.int32)[None, :]
    inside = (offsets >= gap_rows[:, 0:1]) & (offsets < gap_rows[:, 1:2])
    return jnp.where(inside, 0.0, 1.0).astype(jnp.float32).reshape(-1)

def forward_shift(values, offset):
    filler = jnp.zeros((abs(offset), values.shape[1]), values.dtype)
    if offset > 0:
        return jnp.concatenate([values[offset:], filler], 0)
    return jnp.concatenate([filler, values[:offset]], 0)

def norm_part(inputs, valid, gain):
    scaled = inputs.astype(jnp.float32)
    inv_rms = lax.rsqrt(lax.optimization_barrier(jnp.mean(scaled * scaled, axis=-1, keepdims=True)) + EPS)
    return (scaled, inv_rms, scaled * inv_rms * gain * valid[:, None])

def project(preactivation, weight):
    hidden = jax.nn.gelu(preactivation).astype(jnp.bfloat16)
    proj_out = jnp.dot(hidden, weight, preferred_element_type=jnp.float32)
    halfway = weight.shape[1] // 2
    return (hidden, proj_out[:, :halfway], jax.nn.sigmoid(proj_out[:, halfway:]))

def one_track(pair, valid, conv_taps, norm_gains, projection):
    current, grad_in = pair
    stored = []
    for layer in range(LAYERS):
        filter_weight = conv_taps[layer]
        scaled, inv_rms, normalized_tracks = norm_part(current, valid, norm_gains[layer])
        preactivation = filter_weight[0] * forward_shift(normalized_tracks, -DILATION_BINS) + filter_weight[1] * normalized_tracks + filter_weight[2] * forward_shift(normalized_tracks, DILATION_BINS)
        hidden, first, gate = project(preactivation, projection[layer])
        current = (scaled + valid[:, None] * first * gate).astype(jnp.bfloat16)
        stored.append((scaled, inv_rms, normalized_tracks, preactivation, hidden, first, gate))
    grad = grad_in.astype(jnp.float32)
    proj_terms, filter_tap_products, gain_terms = ([], [], [])
    for layer in reversed(range(LAYERS)):
        scaled, inv_rms, normalized_tracks, preactivation, hidden, first, gate = stored[layer]
        filter_weight = conv_taps[layer]
        branch = valid[:, None] * grad
        dproj = jnp.concatenate([branch * gate, branch * first * gate * (1.0 - gate)], 1).astype(jnp.bfloat16)
        dhidden = lax.dot_general(dproj, projection[layer], (((1,), (1,)), ((), ())), preferred_element_type=jnp.float32)
        proj_terms.append(lax.dot_general(hidden, dproj, (((0,), (0,)), ((), ())), preferred_element_type=jnp.float32))
        preactivation_gradient = jax.vjp(jax.nn.gelu, preactivation)[1](dhidden)[0]
        normalized_gradient = filter_weight[0] * forward_shift(preactivation_gradient, DILATION_BINS) + filter_weight[1] * preactivation_gradient + filter_weight[2] * forward_shift(preactivation_gradient, -DILATION_BINS)
        filter_tap_products.append(jnp.stack([lax.optimization_barrier(jnp.sum(preactivation_gradient * forward_shift(normalized_tracks, -DILATION_BINS), 0)), lax.optimization_barrier(jnp.sum(preactivation_gradient * normalized_tracks, 0)), lax.optimization_barrier(jnp.sum(preactivation_gradient * forward_shift(normalized_tracks, DILATION_BINS), 0))]))
        dq = normalized_gradient * valid[:, None]
        gain_terms.append(lax.optimization_barrier(jnp.sum(dq * scaled * inv_rms, 0)))
        dt = dq * norm_gains[layer]
        grad = grad + inv_rms * dt - scaled * inv_rms ** 3 * lax.optimization_barrier(jnp.mean(dt * scaled, axis=-1, keepdims=True))
    return (grad.astype(jnp.bfloat16), jnp.stack(proj_terms[::-1]), jnp.stack(filter_tap_products[::-1]), jnp.stack(gain_terms[::-1]))

def reference(tokens, cotangent, gaps, conv_taps, norm_gains, projection):
    valid = valid_of(gaps)
    results = lax.map(lambda pair: one_track(pair, valid, conv_taps, norm_gains, projection), (tokens, cotangent))
    tokens_grad, proj_terms, filter_tap_products, gain_terms = results
    return (tokens_grad, lax.optimization_barrier(jnp.sum(proj_terms, 0)), lax.optimization_barrier(jnp.sum(filter_tap_products, 0)), lax.optimization_barrier(jnp.sum(gain_terms, 0)))
```

```python
import jax
import jax.numpy as jnp
from jax import lax
from jax.experimental import pallas as pl
from jax.experimental.pallas import tpu as pltpu
from jax.sharding import Mesh
from jax.sharding import PartitionSpec as P

C = 512
DIL = 32
EPS = 1e-06
F32 = jnp.float32
BF16 = jnp.bfloat16
NEAR = ("zl", "xl", "yl")
FAR = ("zh", "xh", "yh")
SEQ = ("zh", "zl", "xh", "xl", "yh")
HAP = ("yl", "c")
G0 = 0.7978845608028654
G1 = 0.044715
PACK = 208
ACT = 144


def gelu_and_slope(x):
    x2 = x * x
    t = jnp.tanh(G0 * x * (1.0 + G1 * x2))
    cdf = 0.5 + 0.5 * t
    slope = cdf + (0.5 * G0) * x * (1.0 - t * t) * (1.0 + (3.0 * G1) * x2)
    return x * cdf, slope


def sigmoid(x):
    return 0.5 + 0.5 * jnp.tanh(0.5 * x)


def dot(a, b, dims):
    return lax.dot_general(a, b, (dims, ((), ())), preferred_element_type=F32)


def fold8(v):
    return jnp.sum(v.reshape(v.shape[0] // 8, 8, v.shape[1]), axis=0)


def hi_lo(v):
    hi = v.astype(BF16)
    lo = (v - hi.astype(F32)).astype(BF16)
    return hi, lo


def body(prev, nxt, tok, cot, own_gap, taps, gains, proj, out, keep, send,
         n0, i0, g0, h0, ab0, x1, n1, i1, g1, h1, po1, dp1, dh1, gr1, dp0, dh0, act):
    core = lax.axis_index("c")
    steps = lax.broadcasted_iota(jnp.int32, (DIL, 1), 0).astype(F32)

    gap_of = []
    for tile in (prev[192:208, :], own_gap[...], nxt[192:208, :]):
        tile = tile.astype(F32)
        gap_of.append((tile[0:1, 0:1], 128.0 - tile[1:2, 0:1]))

    def rows(base, count=DIL):
        ref, at = ((prev, base), (tok, base - 128), (nxt, base - 256))[base // 128]
        return ref[at:at + count, :].astype(F32)

    def cot_rows(base):
        if base < 128:
            return prev[128 + base - 64:128 + base - 32, :].astype(F32)
        if base < 256:
            return cot[base - 128:base - 96, :].astype(F32)
        return nxt[128 + base - 256:128 + base - 224, :].astype(F32)

    valid_of = []
    for chunk in range(12):
        start, end = gap_of[chunk // 4]
        at = steps + float(DIL * (chunk % 4))
        valid_of.append(jnp.where((at >= start) & (at < end), 0.0, 1.0))

    def norm(v, valid, gain):
        inv = lax.rsqrt(jnp.sum(v * v, axis=-1, keepdims=True) * (1.0 / C) + EPS)
        return inv, v * inv * gain * valid

    def tap(layer, k):
        return taps[layer, k:k + 1, :]

    def conv(ref, at, layer):
        return (tap(layer, 0) * ref[at - DIL:at, :] + tap(layer, 1) * ref[at:at + DIL, :]
                + tap(layer, 2) * ref[at + DIL:at + 2 * DIL, :])

    for c in range(12):
        inv, normed = norm(rows(c * DIL), valid_of[c], gains[0:1, :])
        i0[c * DIL:(c + 1) * DIL, :] = inv
        n0[c * DIL:(c + 1) * DIL, :] = normed
    for c in range(1, 11):
        hid, slope = gelu_and_slope(conv(n0, c * DIL, 0))
        h0[(c - 1) * DIL:c * DIL, :] = hid.astype(BF16)
        g0[(c - 1) * DIL:c * DIL, :] = slope
    ab0[...] = dot(h0[...], proj[0], ((1,), (0,)))
    for c in range(1, 11):
        at = slice((c - 1) * DIL, c * DIL)
        first = ab0[at, 0:C]
        gate = sigmoid(ab0[at, C:2 * C])
        both = first * gate
        nx = (rows(c * DIL) + valid_of[c] * both).astype(BF16).astype(F32)
        ab0[at, 0:C] = gate
        ab0[at, C:2 * C] = both * (1.0 - gate)
        inv, normed = norm(nx, valid_of[c], gains[1:2, :])
        x1[at, :] = nx
        i1[at, :] = inv
        n1[at, :] = normed
    for c in range(2, 10):
        hid, slope = gelu_and_slope(conv(n1, (c - 1) * DIL, 1))
        h1[(c - 2) * DIL:(c - 1) * DIL, :] = hid.astype(BF16)
        g1[(c - 2) * DIL:(c - 1) * DIL, :] = slope
    po1[...] = dot(h1[...], proj[1], ((1,), (0,)))
    for c in range(2, 10):
        at = slice((c - 2) * DIL, (c - 1) * DIL)
        first = po1[at, 0:C]
        gate = sigmoid(po1[at, C:2 * C])
        bg = valid_of[c] * cot_rows(c * DIL) * gate
        dp1[at, 0:C] = bg.astype(BF16)
        dp1[at, C:2 * C] = (bg * first * (1.0 - gate)).astype(BF16)
    dh1[...] = dot(dp1[...], proj[1], ((1,), (1,)))
    for c in range(8):
        at = slice(c * DIL, (c + 1) * DIL)
        dh1[at, :] = dh1[at, :] * g1[at, :]

    def back(dref, c_off, layer, c, sref_rows, inv, valid, gain):
        at = c_off
        dn = (tap(layer, 0) * dref[at + DIL:at + 2 * DIL, :] + tap(layer, 1) * dref[at:at + DIL, :]
              + tap(layer, 2) * dref[at - DIL:at, :])
        dq = dn * valid
        si = sref_rows * inv
        qs = dq * si
        dt = dq * gain
        m = jnp.sum(qs * gain, axis=-1, keepdims=True) * (1.0 / C)
        return inv * (dt - si * m), qs

    def small_rows(parts):
        return [jnp.sum(p, axis=0, keepdims=True) for p in parts]

    acc = [jnp.zeros((8, C), F32) for _ in range(4)]
    for c in range(3, 9):
        at1 = slice((c - 1) * DIL, c * DIL)
        delta, qs = back(dh1, (c - 2) * DIL, 1, c, x1[at1, :], i1[at1, :], valid_of[c], gains[1:2, :])
        grad = cot_rows(c * DIL) + delta
        branch = valid_of[c] * grad
        to = slice((c - 3) * DIL, (c - 2) * DIL)
        dp0[to, 0:C] = (branch * ab0[at1, 0:C]).astype(BF16)
        dp0[to, C:2 * C] = (branch * ab0[at1, C:2 * C]).astype(BF16)
        if 4 <= c < 8:
            gr1[(c - 4) * DIL:(c - 3) * DIL, :] = grad
            d = dh1[(c - 2) * DIL:(c - 1) * DIL, :]
            for k in range(3):
                acc[k] += fold8(d * n1[(c - 2 + k) * DIL:(c - 1 + k) * DIL, :])
            acc[3] += fold8(qs)

    def put(layer, hid, dpr, parts):
        act[layer, 0:128, 0:C] = hid
        act[layer, 0:128, C:3 * C] = dpr
        four = jnp.concatenate(small_rows(parts) + [jnp.zeros((12, C), F32)], axis=0)
        hi, lo = hi_lo(four)
        act[layer, 128:ACT, 0:C] = hi
        act[layer, 128:ACT, C:2 * C] = lo
        act[layer, 128:ACT, 2 * C:3 * C] = jnp.zeros((16, C), BF16)

    put(1, h1[64:192, :], dp1[64:192, :], acc)

    dh0[...] = dot(dp0[...], proj[0], ((1,), (1,)))
    for c in range(6):
        at = slice(c * DIL, (c + 1) * DIL)
        dh0[at, :] = dh0[at, :] * g0[(c + 2) * DIL:(c + 3) * DIL, :]
    acc = [jnp.zeros((8, C), F32) for _ in range(4)]
    for c in range(4, 8):
        delta, qs = back(dh0, (c - 3) * DIL, 0, c, rows(c * DIL), i0[c * DIL:(c + 1) * DIL, :],
                         valid_of[c], gains[0:1, :])
        at = slice((c - 4) * DIL, (c - 3) * DIL)
        out[at, :] = (gr1[at, :] + delta).astype(BF16)
        d = dh0[(c - 3) * DIL:(c - 2) * DIL, :]
        for k in range(3):
            acc[k] += fold8(d * n0[(c - 1 + k) * DIL:(c + k) * DIL, :])
        acc[3] += fold8(qs)
    put(0, h0[96:224, :], dp0[32:160, :], acc)
    keep[...] = act[core]
    send[...] = act[1 - core]


def terms(keep, recv, out):
    q = lax.broadcasted_iota(jnp.int32, (C, 1), 0)
    ch = (((q >> 4) & 3) << 7 | ((q >> 8) & 1) << 6 | ((q >> 3) & 1) << 5 | ((q >> 7) & 1) << 4
          | ((q >> 1) & 3) << 2 | ((q >> 6) & 1) << 1 | (q & 1))
    pick = (ch == lax.broadcasted_iota(jnp.int32, (C, C), 1)).astype(F32).astype(BF16)
    ha = dot(pick, keep[0:128, 0:C], ((1,), (1,))).astype(BF16)
    hb = dot(pick, recv[0:128, 0:C], ((1,), (1,))).astype(BF16)
    for j in range(8):
        cols = slice(C + j * 128, C + (j + 1) * 128)
        t = dot(ha, keep[0:128, cols], ((1,), (0,))) + dot(hb, recv[0:128, cols], ((1,), (0,)))
        out[:, j * 64:(j + 1) * 64, :] = t.astype(BF16).reshape(8, 64, 128)
    small = (keep[128:ACT, 0:C].astype(F32) + keep[128:ACT, C:2 * C].astype(F32)
             + recv[128:ACT, 0:C].astype(F32) + recv[128:ACT, C:2 * C].astype(F32))
    pad = jnp.zeros((12, 128), F32)
    for g in range(8):
        row, half = g // 2, (g % 2) * 256
        two = jnp.concatenate([small[row:row + 1, half + 128 * m:half + 128 * (m + 1)] for m in range(2)], axis=0)
        hi = two.astype(BF16).astype(F32)
        out[g, 512:528, :] = jnp.concatenate([hi, two - hi, pad], axis=0).astype(BF16)


def first_sum(recv, out):
    total = recv[0].astype(F32)
    for i in range(1, 8):
        total += recv[i].astype(F32)
    p = lax.broadcasted_iota(jnp.int32, (C, 1), 0)
    src = ((p >> 1) & 7) << 6 | (p >> 4) << 1 | (p & 1)
    pick = (src == lax.broadcasted_iota(jnp.int32, (C, C), 1)).astype(F32).astype(BF16)
    moved = dot(pick, total[0:512, :].astype(BF16), ((1,), (0,))).astype(BF16)
    out[:, 0:16, :] = moved.reshape(32, 16, 128)
    two = total[512:514, :] + total[514:516, :]
    hi = two.astype(BF16).astype(F32)
    tile = jnp.concatenate([hi, two - hi, jnp.zeros((12, 128), F32)], axis=0).astype(BF16)
    for d in range(32):
        out[d, 16:32, :] = tile


def second_sum(recv, out):
    total = recv[0].astype(F32)
    for i in range(1, 32):
        total += recv[i].astype(F32)
    two = total[16:18, :] + total[18:20, :]
    both = jnp.concatenate([total[0:16, :], two, jnp.zeros((6, 128), F32)], axis=0)
    for i in range(16):
        out[i] = both


def place(recv, proj, taps, gains):
    base = (lax.axis_index("zl") * 2 + lax.axis_index("xl")) * 4
    for c in range(2):
        for y in range(2):
            piece = recv[base + y * 2 + c]
            for j in range(8):
                proj[c, 2 * y:2 * y + 2, j * 128:(j + 1) * 128] = piece[2 * j:2 * j + 2, :]
        for g in range(8):
            two = recv[g * 2 + c, 16:24, :]
            for m in range(2):
                cols = slice((g % 2) * 256 + m * 128, (g % 2) * 256 + (m + 1) * 128)
                if g < 6:
                    taps[c, g // 2:g // 2 + 1, cols] = two[m:m + 1, :]
                else:
                    gains[c:c + 1, cols] = two[m:m + 1, :]


def call(kernel, outs, scratch=(), **kw):
    single = not isinstance(outs, (list, tuple))
    return pl.pallas_call(
        kernel,
        out_shape=outs,
        out_specs=pl.BlockSpec(memory_space=pltpu.VMEM) if single
        else [pl.BlockSpec(memory_space=pltpu.VMEM)] * len(outs),
        scratch_shapes=list(scratch),
        compiler_params=pltpu.CompilerParams(vmem_limit_bytes=48 * 1024 * 1024),
        **kw,
    )


def shards(tokens, cotangent, gaps, taps, gains, proj):
    tok, cot = tokens[0], cotangent[0]
    pair = jnp.stack([gaps[0, 0], 128 - gaps[0, 1]]).astype(BF16)
    own_gap = jnp.pad(jnp.broadcast_to(pair[:, None], (2, C)), ((0, 14), (0, 0)))
    n = 128
    up = jnp.concatenate([tok, cot[64:], own_gap], axis=0)
    down = jnp.concatenate([tok, cot[:64], own_gap], axis=0)
    prev = lax.ppermute(up, SEQ, [(i, i + 1) for i in range(n - 1)])
    nxt = lax.ppermute(down, SEQ, [(i + 1, i) for i in range(n - 1)])
    s = jax.ShapeDtypeStruct
    v = pltpu.VMEM
    tokens_grad, keep, send = call(
        body,
        [s((128, C), BF16), s((ACT, 3 * C), BF16), s((ACT, 3 * C), BF16)],
        [v((384, C), F32), v((384, 1), F32), v((320, C), F32), v((320, C), BF16), v((320, 2 * C), F32),
         v((320, C), F32), v((320, C), F32), v((320, 1), F32), v((256, C), F32), v((256, C), BF16),
         v((256, 2 * C), F32), v((256, 2 * C), BF16), v((256, C), F32), v((128, C), F32),
         v((192, 2 * C), BF16), v((192, C), F32), v((2, ACT, 3 * C), BF16)],
    )(prev, nxt, tok, cot, own_gap, taps, gains, proj)
    recv = lax.ppermute(send, "c", [(0, 1), (1, 0)])
    part = call(terms, s((8, 528, 128), BF16))(keep, recv)
    part = lax.all_to_all(part, NEAR, 0, 0, tiled=True)
    part = call(first_sum, s((32, 32, 128), BF16))(part)
    part = lax.all_to_all(part, FAR, 0, 0, tiled=True)
    part = call(second_sum, s((16, 24, 128), F32))(part)
    part = lax.all_to_all(part, NEAR + ("c",), 0, 0, tiled=True)
    projection_grad, taps_grad, gains_grad = call(
        place, [s((2, 4, 1024), F32), s((2, 3, C), F32), s((2, C), F32)]
    )(part)
    return tokens_grad[None], projection_grad, taps_grad, gains_grad


def solution(mesh):
    fine = Mesh(mesh.devices.reshape(4, 2, 2, 2, 4, 2, 2), ("zh", "zl", "xh", "xl", "yh", "yl", "c"))
    return jax.shard_map(
        shards,
        mesh=fine,
        in_specs=(P(HAP, SEQ, None), P(HAP, SEQ, None), P(SEQ, None), P(), P(), P()),
        out_specs=(P(HAP, SEQ, None), P(None, SEQ, None), P(), P()),
        check_vma=False,
    )
```

```python
import jax
import jax.numpy as jnp
from jax import lax
from jax.experimental import pallas as pl
from jax.experimental.pallas import tpu as pltpu
from jax.sharding import Mesh
from jax.sharding import PartitionSpec as P

C = 512
DIL = 32
EPS = 1e-06
F32 = jnp.float32
BF16 = jnp.bfloat16
NEAR = ("zl", "xl", "yl")
FAR = ("zh", "xh", "yh")
SEQ = ("zh", "zl", "xh", "xl", "yh")
HAP = ("yl", "c")
G0 = 0.7978845608028654
G1 = 0.044715
MARK = 64.0
ACT = 144


def gelu_and_slope(x):
    x2 = x * x
    t = jnp.tanh(G0 * x * (1.0 + G1 * x2))
    cdf = 0.5 + 0.5 * t
    slope = cdf + (0.5 * G0) * x * (1.0 - t * t) * (1.0 + (3.0 * G1) * x2)
    return x * cdf, slope


def sigmoid(x):
    return 0.5 + 0.5 * jnp.tanh(0.5 * x)


def dot(a, b, dims):
    return lax.dot_general(a, b, (dims, ((), ())), preferred_element_type=F32)


def fold8(v):
    return jnp.sum(v.reshape(v.shape[0] // 8, 8, v.shape[1]), axis=0)


def hi_lo(v):
    hi = v.astype(BF16)
    lo = (v - hi.astype(F32)).astype(BF16)
    return hi, lo


def pack(gaps, tok, cot, up, down):
    at = lax.broadcasted_iota(jnp.int32, (128, 1), 0)
    inside = (at >= gaps[0, 0]) & (at < gaps[0, 1])
    marked = jnp.where(inside, MARK, tok[...].astype(F32)).astype(BF16)
    up[0:128, :] = marked
    down[0:128, :] = marked
    up[128:192, :] = cot[64:128, :]
    down[128:192, :] = cot[0:64, :]


def warm(gaps, tok, cot, taps, gains, proj, valid, tok_out, cot_out, taps_out, gains_out, proj_out):
    at = lax.broadcasted_iota(jnp.int32, (128, 1), 0)
    valid[...] = jnp.where((at >= gaps[0, 0]) & (at < gaps[0, 1]), 0.0, 1.0)
    for a, b in ((tok, tok_out), (cot, cot_out), (taps, taps_out), (gains, gains_out), (proj, proj_out)):
        b[...] = a[...]


def body(own_valid, prev, nxt, tok, cot, taps, gains, proj, out, keep, send,
         n0, i0, g0, h0, ab0, x1, n1, i1, g1, h1, po1, dp1, dh1, gr1, dp0, dh0, act):
    core = lax.axis_index("c")
    place_in_seq = sum(lax.axis_index(a) for a in SEQ)
    inner = (place_in_seq > 0, None, place_in_seq < 9)

    def rows(base):
        ref, at = ((prev, base), (tok, base - 128), (nxt, base - 256))[base // 128]
        v = ref[at:at + DIL, :].astype(F32)
        return v if ref is tok else jnp.where(v[:, 0:1] < 0.5 * MARK, v, 0.0)

    def cot_rows(base):
        if base < 128:
            return prev[128 + base - 64:128 + base - 32, :].astype(F32)
        if base < 256:
            return cot[base - 128:base - 96, :].astype(F32)
        return nxt[128 + base - 256:128 + base - 224, :].astype(F32)

    valid_of = []
    for chunk in range(12):
        if 4 <= chunk < 8:
            valid_of.append(own_valid[DIL * (chunk - 4):DIL * (chunk - 3), :])
        else:
            ref = prev if chunk < 4 else nxt
            lead = ref[DIL * (chunk % 4):DIL * (chunk % 4) + DIL, 0:128].astype(F32)[:, 0:1]
            valid_of.append(jnp.where(lead < 0.5 * MARK, jnp.where(inner[chunk // 4], 1.0, 0.0), 0.0))

    def norm(v, valid, gain):
        inv = lax.rsqrt(jnp.sum(v * v, axis=-1, keepdims=True) * (1.0 / C) + EPS)
        return inv, v * inv * gain * valid

    def tap(layer, k):
        return taps[k, layer:layer + 1, :]

    def conv(ref, at, layer):
        return (tap(layer, 0) * ref[at - DIL:at, :] + tap(layer, 1) * ref[at:at + DIL, :]
                + tap(layer, 2) * ref[at + DIL:at + 2 * DIL, :])

    for c in range(12):
        inv, normed = norm(rows(c * DIL), valid_of[c], gains[0:1, :])
        i0[c * DIL:(c + 1) * DIL, :] = inv
        n0[c * DIL:(c + 1) * DIL, :] = normed
    for c in range(1, 11):
        hid, slope = gelu_and_slope(conv(n0, c * DIL, 0))
        h0[(c - 1) * DIL:c * DIL, :] = hid.astype(BF16)
        g0[(c - 1) * DIL:c * DIL, :] = slope
    ab0[...] = dot(h0[...], proj[0], ((1,), (0,)))
    for c in range(1, 11):
        at = slice((c - 1) * DIL, c * DIL)
        first = ab0[at, 0:C]
        gate = sigmoid(ab0[at, C:2 * C])
        both = first * gate
        nx = (rows(c * DIL) + valid_of[c] * both).astype(BF16).astype(F32)
        ab0[at, 0:C] = gate
        ab0[at, C:2 * C] = both * (1.0 - gate)
        inv, normed = norm(nx, valid_of[c], gains[1:2, :])
        x1[at, :] = nx
        i1[at, :] = inv
        n1[at, :] = normed
    for c in range(2, 10):
        hid, slope = gelu_and_slope(conv(n1, (c - 1) * DIL, 1))
        h1[(c - 2) * DIL:(c - 1) * DIL, :] = hid.astype(BF16)
        g1[(c - 2) * DIL:(c - 1) * DIL, :] = slope
    po1[...] = dot(h1[...], proj[1], ((1,), (0,)))
    for c in range(2, 10):
        at = slice((c - 2) * DIL, (c - 1) * DIL)
        first = po1[at, 0:C]
        gate = sigmoid(po1[at, C:2 * C])
        bg = valid_of[c] * cot_rows(c * DIL) * gate
        dp1[at, 0:C] = bg.astype(BF16)
        dp1[at, C:2 * C] = (bg * first * (1.0 - gate)).astype(BF16)
    dh1[...] = dot(dp1[...], proj[1], ((1,), (1,)))
    for c in range(8):
        at = slice(c * DIL, (c + 1) * DIL)
        dh1[at, :] = dh1[at, :] * g1[at, :]

    def back(dref, c_off, layer, c, sref_rows, inv, valid, gain):
        at = c_off
        dn = (tap(layer, 0) * dref[at + DIL:at + 2 * DIL, :] + tap(layer, 1) * dref[at:at + DIL, :]
              + tap(layer, 2) * dref[at - DIL:at, :])
        dq = dn * valid
        si = sref_rows * inv
        qs = dq * si
        dt = dq * gain
        m = jnp.sum(qs * gain, axis=-1, keepdims=True) * (1.0 / C)
        return inv * (dt - si * m), qs

    def small_rows(parts):
        return [jnp.sum(p, axis=0, keepdims=True) for p in parts]

    acc = [jnp.zeros((8, C), F32) for _ in range(4)]
    for c in range(3, 9):
        at1 = slice((c - 1) * DIL, c * DIL)
        delta, qs = back(dh1, (c - 2) * DIL, 1, c, x1[at1, :], i1[at1, :], valid_of[c], gains[1:2, :])
        grad = cot_rows(c * DIL) + delta
        branch = valid_of[c] * grad
        to = slice((c - 3) * DIL, (c - 2) * DIL)
        dp0[to, 0:C] = (branch * ab0[at1, 0:C]).astype(BF16)
        dp0[to, C:2 * C] = (branch * ab0[at1, C:2 * C]).astype(BF16)
        if 4 <= c < 8:
            gr1[(c - 4) * DIL:(c - 3) * DIL, :] = grad
            d = dh1[(c - 2) * DIL:(c - 1) * DIL, :]
            for k in range(3):
                acc[k] += fold8(d * n1[(c - 2 + k) * DIL:(c - 1 + k) * DIL, :])
            acc[3] += fold8(qs)

    def put(layer, hid, dpr, parts):
        act[layer, 0:128, 0:C] = hid
        act[layer, 0:128, C:3 * C] = dpr
        four = jnp.concatenate(small_rows(parts) + [jnp.zeros((12, C), F32)], axis=0)
        hi, lo = hi_lo(four)
        act[layer, 128:ACT, 0:C] = hi
        act[layer, 128:ACT, C:2 * C] = lo
        act[layer, 128:ACT, 2 * C:3 * C] = jnp.zeros((16, C), BF16)

    put(1, h1[64:192, :], dp1[64:192, :], acc)

    dh0[...] = dot(dp0[...], proj[0], ((1,), (1,)))
    for c in range(6):
        at = slice(c * DIL, (c + 1) * DIL)
        dh0[at, :] = dh0[at, :] * g0[(c + 2) * DIL:(c + 3) * DIL, :]
    acc = [jnp.zeros((8, C), F32) for _ in range(4)]
    for c in range(4, 8):
        delta, qs = back(dh0, (c - 3) * DIL, 0, c, rows(c * DIL), i0[c * DIL:(c + 1) * DIL, :],
                         valid_of[c], gains[0:1, :])
        at = slice((c - 4) * DIL, (c - 3) * DIL)
        out[at, :] = (gr1[at, :] + delta).astype(BF16)
        d = dh0[(c - 3) * DIL:(c - 2) * DIL, :]
        for k in range(3):
            acc[k] += fold8(d * n0[(c - 1 + k) * DIL:(c + k) * DIL, :])
        acc[3] += fold8(qs)
    put(0, h0[96:224, :], dp0[32:160, :], acc)
    keep[...] = act[core]
    send[...] = act[1 - core]


def terms(keep, recv, out):
    q = lax.broadcasted_iota(jnp.int32, (C, 1), 0)
    ch = (((q >> 4) & 3) << 7 | ((q >> 8) & 1) << 6 | ((q >> 3) & 1) << 5 | ((q >> 7) & 1) << 4
          | ((q >> 1) & 3) << 2 | ((q >> 6) & 1) << 1 | (q & 1))
    pick = (ch == lax.broadcasted_iota(jnp.int32, (C, C), 1)).astype(F32).astype(BF16)
    ha = dot(pick, keep[0:128, 0:C], ((1,), (1,))).astype(BF16)
    hb = dot(pick, recv[0:128, 0:C], ((1,), (1,))).astype(BF16)
    for j in range(8):
        cols = slice(C + j * 128, C + (j + 1) * 128)
        t = dot(ha, keep[0:128, cols], ((1,), (0,))) + dot(hb, recv[0:128, cols], ((1,), (0,)))
        out[:, j * 64:(j + 1) * 64, :] = t.astype(BF16).reshape(8, 64, 128)
    small = (keep[128:ACT, 0:C].astype(F32) + keep[128:ACT, C:2 * C].astype(F32)
             + recv[128:ACT, 0:C].astype(F32) + recv[128:ACT, C:2 * C].astype(F32))
    tile = jnp.concatenate(
        [small[r:r + 1, 128 * q:128 * (q + 1)] for r in range(4) for q in range(4)], axis=0).astype(BF16)
    for g in range(8):
        out[g, 512:528, :] = tile


def first_sum(recv, out):
    total = recv[0].astype(F32)
    for i in range(1, 8):
        total += recv[i].astype(F32)
    p = lax.broadcasted_iota(jnp.int32, (C, 1), 0)
    src = ((p >> 1) & 7) << 6 | (p >> 4) << 1 | (p & 1)
    pick = (src == lax.broadcasted_iota(jnp.int32, (C, C), 1)).astype(F32).astype(BF16)
    moved = dot(pick, total[0:512, :].astype(BF16), ((1,), (0,))).astype(BF16)
    out[:, 0:16, :] = moved.reshape(32, 16, 128)
    tile = total[512:528, :].astype(BF16)
    for d in range(32):
        out[d, 16:32, :] = tile


def second_sum(recv, out):
    total = recv[0].astype(F32)
    for i in range(1, 32):
        total += recv[i].astype(F32)
    out[...] = total


def place(recv, proj, taps, gains):
    for c in range(2):
        for y in range(2):
            for j in range(8):
                proj[c, 2 * y:2 * y + 2, j * 128:(j + 1) * 128] = recv[y * 2 + c, 2 * j:2 * j + 2, :]
        for r in range(4):
            for q in range(4):
                row = recv[c, 16 + r * 4 + q:17 + r * 4 + q, :]
                if r < 3:
                    taps[r, c:c + 1, q * 128:(q + 1) * 128] = row
                else:
                    gains[c:c + 1, q * 128:(q + 1) * 128] = row


def call(kernel, ins, outs, scratch=(), mib=48):
    single = not isinstance(outs, (list, tuple))
    vmem = pl.BlockSpec(memory_space=pltpu.VMEM)
    return pl.pallas_call(
        kernel,
        out_shape=outs,
        in_specs=[pl.BlockSpec(memory_space={"v": pltpu.VMEM, "s": pltpu.SMEM, "a": pl.ANY}[m]) for m in ins],
        out_specs=vmem if single else [vmem] * len(outs),
        scratch_shapes=list(scratch),
        compiler_params=pltpu.CompilerParams(vmem_limit_bytes=int(mib * 1024 * 1024)),
    )


def shards(tokens, cotangent, gaps, taps, gains, proj):
    tok, cot = tokens[0], cotangent[0]
    n = 128
    s = jax.ShapeDtypeStruct
    v = pltpu.VMEM
    up, down = call(pack, "svv", [s((192, C), BF16), s((192, C), BF16)], mib=58)(gaps, tok, cot)
    prev = lax.ppermute(up, SEQ, [(i, i + 1) for i in range(n - 1)])
    nxt = lax.ppermute(down, SEQ, [(i + 1, i) for i in range(n - 1)])
    near_args = call(
        warm,
        "svvvvv",
        [s((128, 1), F32), s((128, C), BF16), s((128, C), BF16), s((3, 2, C), F32), s((2, C), F32),
         s((2, C, 2 * C), BF16)],
    )(gaps, tok, cot, jnp.transpose(taps, (1, 0, 2)), gains, proj)
    tokens_grad, keep, send = call(
        body,
        "vvvvvvvv",
        [s((128, C), BF16), s((ACT, 3 * C), BF16), s((ACT, 3 * C), BF16)],
        [v((384, C), F32), v((384, 1), F32), v((320, C), F32), v((320, C), BF16), v((320, 2 * C), F32),
         v((320, C), F32), v((320, C), F32), v((320, 1), F32), v((256, C), F32), v((256, C), BF16),
         v((256, 2 * C), F32), v((256, 2 * C), BF16), v((256, C), F32), v((128, C), F32),
         v((192, 2 * C), BF16), v((192, C), F32), v((2, ACT, 3 * C), BF16)],
    )(near_args[0], prev, nxt, *near_args[1:])
    recv = lax.ppermute(send, "c", [(0, 1), (1, 0)])
    part = call(terms, "vv", s((8, 528, 128), BF16))(keep, recv)
    part = lax.all_to_all(part, NEAR, 0, 0, tiled=True)
    part = call(first_sum, "v", s((32, 32, 128), BF16))(part)
    part = lax.all_to_all(part, FAR, 0, 0, tiled=True)
    part = call(second_sum, "v", s((32, 128), F32))(part)
    part = lax.all_gather(part, HAP, axis=0)
    projection_grad, taps_grad, gains_grad = call(
        place, "v", [s((2, 4, 1024), F32), s((3, 2, C), F32), s((2, C), F32)]
    )(part)
    return tokens_grad[None], projection_grad, jnp.transpose(taps_grad, (1, 0, 2)), gains_grad


def solution(mesh):
    fine = Mesh(mesh.devices.reshape(4, 2, 2, 2, 4, 2, 2), ("zh", "zl", "xh", "xl", "yh", "yl", "c"))
    return jax.shard_map(
        shards,
        mesh=fine,
        in_specs=(P(HAP, SEQ, None), P(HAP, SEQ, None), P(SEQ, None), P(), P(), P()),
        out_specs=(P(HAP, SEQ, None), P(None, SEQ, None), P(), P()),
        check_vma=False,
    )
```

```python
import jax
import jax.numpy as jnp
from jax import lax
from jax.experimental import pallas as pl
from jax.experimental.pallas import tpu as pltpu
from jax.sharding import Mesh
from jax.sharding import PartitionSpec as P

C = 512
DIL = 32
EPS = 1e-06
F32 = jnp.float32
BF16 = jnp.bfloat16
NEAR = ("x", "yl")
FAR = ("z", "yh")
SEQ = ("z", "x", "yh")
HAP = ("yl", "c")
G0 = 0.7978845608028654
G1 = 0.044715
MARK = 64.0
ACT = 144


def gelu_and_slope(x):
    x2 = x * x
    t = jnp.tanh(G0 * x * (1.0 + G1 * x2))
    cdf = 0.5 + 0.5 * t
    slope = cdf + (0.5 * G0) * x * (1.0 - t * t) * (1.0 + (3.0 * G1) * x2)
    return x * cdf, slope


def sigmoid(x):
    return 0.5 + 0.5 * jnp.tanh(0.5 * x)


def dot(a, b, dims):
    return lax.dot_general(a, b, (dims, ((), ())), preferred_element_type=F32)


def fold8(v):
    return jnp.sum(v.reshape(v.shape[0] // 8, 8, v.shape[1]), axis=0)


def hi_lo(v):
    hi = v.astype(BF16)
    lo = (v - hi.astype(F32)).astype(BF16)
    return hi, lo


def pack(gaps, tok, cot, up, down):
    at = lax.broadcasted_iota(jnp.int32, (128, 1), 0)
    inside = (at >= gaps[0, 0]) & (at < gaps[0, 1])
    marked = jnp.where(inside, MARK, tok[...].astype(F32)).astype(BF16)
    up[0:128, :] = marked
    down[0:128, :] = marked
    up[128:192, :] = cot[64:128, :]
    down[128:192, :] = cot[0:64, :]


def warm(gaps, tok, cot, taps, gains, proj, valid, tok_out, cot_out, taps_out, gains_out, proj_out):
    at = lax.broadcasted_iota(jnp.int32, (128, 1), 0)
    valid[...] = jnp.where((at >= gaps[0, 0]) & (at < gaps[0, 1]), 0.0, 1.0)
    for a, b in ((tok, tok_out), (cot, cot_out), (taps, taps_out), (gains, gains_out), (proj, proj_out)):
        b[...] = a[...]


def body(own_valid, prev, nxt, tok, cot, taps, gains, proj, out, keep, send,
         n0, i0, g0, h0, ab0, x1, n1, i1, g1, h1, po1, dp1, dh1, gr1, dp0, dh0, act):
    core = lax.axis_index("c")
    place_in_seq = sum(lax.axis_index(a) for a in SEQ)
    inner = (place_in_seq > 0, None, place_in_seq < 13)

    def rows(base):
        ref, at = ((prev, base), (tok, base - 128), (nxt, base - 256))[base // 128]
        v = ref[at:at + DIL, :].astype(F32)
        return v if ref is tok else jnp.where(v[:, 0:1] < 0.5 * MARK, v, 0.0)

    def cot_rows(base):
        if base < 128:
            return prev[128 + base - 64:128 + base - 32, :].astype(F32)
        if base < 256:
            return cot[base - 128:base - 96, :].astype(F32)
        return nxt[128 + base - 256:128 + base - 224, :].astype(F32)

    valid_of = []
    for chunk in range(12):
        if 4 <= chunk < 8:
            valid_of.append(own_valid[DIL * (chunk - 4):DIL * (chunk - 3), :])
        else:
            ref = prev if chunk < 4 else nxt
            lead = ref[DIL * (chunk % 4):DIL * (chunk % 4) + DIL, 0:128].astype(F32)[:, 0:1]
            valid_of.append(jnp.where(lead < 0.5 * MARK, jnp.where(inner[chunk // 4], 1.0, 0.0), 0.0))

    def norm(v, valid, gain):
        inv = lax.rsqrt(jnp.sum(v * v, axis=-1, keepdims=True) * (1.0 / C) + EPS)
        return inv, v * inv * gain * valid

    def tap(layer, k):
        return taps[k, layer:layer + 1, :]

    def conv(ref, at, layer):
        return (tap(layer, 0) * ref[at - DIL:at, :] + tap(layer, 1) * ref[at:at + DIL, :]
                + tap(layer, 2) * ref[at + DIL:at + 2 * DIL, :])

    for c in range(12):
        inv, normed = norm(rows(c * DIL), valid_of[c], gains[0:1, :])
        i0[c * DIL:(c + 1) * DIL, :] = inv
        n0[c * DIL:(c + 1) * DIL, :] = normed
    for c in range(1, 11):
        hid, slope = gelu_and_slope(conv(n0, c * DIL, 0))
        h0[(c - 1) * DIL:c * DIL, :] = hid.astype(BF16)
        g0[(c - 1) * DIL:c * DIL, :] = slope
    ab0[...] = dot(h0[...], proj[0], ((1,), (0,)))
    for c in range(1, 11):
        at = slice((c - 1) * DIL, c * DIL)
        first = ab0[at, 0:C]
        gate = sigmoid(ab0[at, C:2 * C])
        both = first * gate
        nx = (rows(c * DIL) + valid_of[c] * both).astype(BF16).astype(F32)
        ab0[at, 0:C] = gate
        ab0[at, C:2 * C] = both * (1.0 - gate)
        inv, normed = norm(nx, valid_of[c], gains[1:2, :])
        x1[at, :] = nx
        i1[at, :] = inv
        n1[at, :] = normed
    for c in range(2, 10):
        hid, slope = gelu_and_slope(conv(n1, (c - 1) * DIL, 1))
        h1[(c - 2) * DIL:(c - 1) * DIL, :] = hid.astype(BF16)
        g1[(c - 2) * DIL:(c - 1) * DIL, :] = slope
    po1[...] = dot(h1[...], proj[1], ((1,), (0,)))
    for c in range(2, 10):
        at = slice((c - 2) * DIL, (c - 1) * DIL)
        first = po1[at, 0:C]
        gate = sigmoid(po1[at, C:2 * C])
        bg = valid_of[c] * cot_rows(c * DIL) * gate
        dp1[at, 0:C] = bg.astype(BF16)
        dp1[at, C:2 * C] = (bg * first * (1.0 - gate)).astype(BF16)
    dh1[...] = dot(dp1[...], proj[1], ((1,), (1,)))
    for c in range(8):
        at = slice(c * DIL, (c + 1) * DIL)
        dh1[at, :] = dh1[at, :] * g1[at, :]

    def back(dref, c_off, layer, c, sref_rows, inv, valid, gain):
        at = c_off
        dn = (tap(layer, 0) * dref[at + DIL:at + 2 * DIL, :] + tap(layer, 1) * dref[at:at + DIL, :]
              + tap(layer, 2) * dref[at - DIL:at, :])
        dq = dn * valid
        si = sref_rows * inv
        qs = dq * si
        dt = dq * gain
        m = jnp.sum(qs * gain, axis=-1, keepdims=True) * (1.0 / C)
        return inv * (dt - si * m), qs

    def small_rows(parts):
        return [jnp.sum(p, axis=0, keepdims=True) for p in parts]

    acc = [jnp.zeros((8, C), F32) for _ in range(4)]
    for c in range(3, 9):
        at1 = slice((c - 1) * DIL, c * DIL)
        delta, qs = back(dh1, (c - 2) * DIL, 1, c, x1[at1, :], i1[at1, :], valid_of[c], gains[1:2, :])
        grad = cot_rows(c * DIL) + delta
        branch = valid_of[c] * grad
        to = slice((c - 3) * DIL, (c - 2) * DIL)
        dp0[to, 0:C] = (branch * ab0[at1, 0:C]).astype(BF16)
        dp0[to, C:2 * C] = (branch * ab0[at1, C:2 * C]).astype(BF16)
        if 4 <= c < 8:
            gr1[(c - 4) * DIL:(c - 3) * DIL, :] = grad
            d = dh1[(c - 2) * DIL:(c - 1) * DIL, :]
            for k in range(3):
                acc[k] += fold8(d * n1[(c - 2 + k) * DIL:(c - 1 + k) * DIL, :])
            acc[3] += fold8(qs)

    def put(layer, hid, dpr, parts):
        act[layer, 0:128, 0:C] = hid
        act[layer, 0:128, C:3 * C] = dpr
        four = jnp.concatenate(small_rows(parts) + [jnp.zeros((12, C), F32)], axis=0)
        hi, lo = hi_lo(four)
        act[layer, 128:ACT, 0:C] = hi
        act[layer, 128:ACT, C:2 * C] = lo
        act[layer, 128:ACT, 2 * C:3 * C] = jnp.zeros((16, C), BF16)

    put(1, h1[64:192, :], dp1[64:192, :], acc)

    dh0[...] = dot(dp0[...], proj[0], ((1,), (1,)))
    for c in range(6):
        at = slice(c * DIL, (c + 1) * DIL)
        dh0[at, :] = dh0[at, :] * g0[(c + 2) * DIL:(c + 3) * DIL, :]
    acc = [jnp.zeros((8, C), F32) for _ in range(4)]
    for c in range(4, 8):
        delta, qs = back(dh0, (c - 3) * DIL, 0, c, rows(c * DIL), i0[c * DIL:(c + 1) * DIL, :],
                         valid_of[c], gains[0:1, :])
        at = slice((c - 4) * DIL, (c - 3) * DIL)
        out[at, :] = (gr1[at, :] + delta).astype(BF16)
        d = dh0[(c - 3) * DIL:(c - 2) * DIL, :]
        for k in range(3):
            acc[k] += fold8(d * n0[(c - 1 + k) * DIL:(c + k) * DIL, :])
        acc[3] += fold8(qs)
    put(0, h0[96:224, :], dp0[32:160, :], acc)
    keep[...] = act[core]
    send[...] = act[1 - core]


def terms(keep, recv, out):
    q = lax.broadcasted_iota(jnp.int32, (C, 1), 0)
    ch = ((q >> 3) & 7) << 6 | ((q >> 7) & 3) << 4 | ((q >> 1) & 3) << 2 | ((q >> 6) & 1) << 1 | (q & 1)
    pick = (ch == lax.broadcasted_iota(jnp.int32, (C, C), 1)).astype(F32).astype(BF16)
    ha = dot(pick, keep[0:128, 0:C], ((1,), (1,))).astype(BF16)
    hb = dot(pick, recv[0:128, 0:C], ((1,), (1,))).astype(BF16)
    for j in range(8):
        cols = slice(C + j * 128, C + (j + 1) * 128)
        t = dot(ha, keep[0:128, cols], ((1,), (0,))) + dot(hb, recv[0:128, cols], ((1,), (0,)))
        out[:, j * 64:(j + 1) * 64, :] = t.astype(BF16).reshape(8, 64, 128)
    small = (keep[128:ACT, 0:C].astype(F32) + keep[128:ACT, C:2 * C].astype(F32)
             + recv[128:ACT, 0:C].astype(F32) + recv[128:ACT, C:2 * C].astype(F32))
    tile = jnp.concatenate(
        [small[r:r + 1, 128 * q:128 * (q + 1)] for r in range(4) for q in range(4)], axis=0).astype(BF16)
    for g in range(8):
        out[g, 512:528, :] = tile


def first_sum(recv, out):
    total = recv[0].astype(F32)
    for i in range(1, 8):
        total += recv[i].astype(F32)
    p = lax.broadcasted_iota(jnp.int32, (C, 1), 0)
    src = ((p >> 1) & 7) << 6 | (p >> 4) << 1 | (p & 1)
    pick = (src == lax.broadcasted_iota(jnp.int32, (C, C), 1)).astype(F32).astype(BF16)
    moved = dot(pick, total[0:512, :].astype(BF16), ((1,), (0,))).astype(BF16)
    out[:, 0:16, :] = moved.reshape(32, 16, 128)
    tile = total[512:528, :].astype(BF16)
    for d in range(32):
        out[d, 16:32, :] = tile


def second_sum(recv, out):
    total = recv[0].astype(F32)
    for i in range(1, 32):
        total += recv[i].astype(F32)
    out[...] = total


def place(recv, proj, taps, gains):
    for c in range(2):
        for y in range(2):
            for j in range(8):
                proj[c, 2 * y:2 * y + 2, j * 128:(j + 1) * 128] = recv[y * 2 + c, 2 * j:2 * j + 2, :]
        for r in range(4):
            for q in range(4):
                row = recv[c, 16 + r * 4 + q:17 + r * 4 + q, :]
                if r < 3:
                    taps[r, c:c + 1, q * 128:(q + 1) * 128] = row
                else:
                    gains[c:c + 1, q * 128:(q + 1) * 128] = row


def call(kernel, ins, outs, scratch=(), mib=48):
    single = not isinstance(outs, (list, tuple))
    vmem = pl.BlockSpec(memory_space=pltpu.VMEM)
    return pl.pallas_call(
        kernel,
        out_shape=outs,
        in_specs=[pl.BlockSpec(memory_space={"v": pltpu.VMEM, "s": pltpu.SMEM, "a": pl.ANY}[m]) for m in ins],
        out_specs=vmem if single else [vmem] * len(outs),
        scratch_shapes=list(scratch),
        compiler_params=pltpu.CompilerParams(vmem_limit_bytes=int(mib * 1024 * 1024)),
    )


def shards(tokens, cotangent, gaps, taps, gains, proj):
    tok, cot = tokens[0], cotangent[0]
    n = 128
    s = jax.ShapeDtypeStruct
    v = pltpu.VMEM
    far = [pltpu.with_memory_space_constraint(a, pltpu.HBM) for a in (gaps, tok, cot)]
    up, down = call(pack, "svv", [s((192, C), BF16), s((192, C), BF16)], mib=48)(*far)
    prev = lax.ppermute(up, SEQ, [(i, i + 1) for i in range(n - 1)])
    nxt = lax.ppermute(down, SEQ, [(i + 1, i) for i in range(n - 1)])
    near_args = call(
        warm,
        "svvvvv",
        [s((128, 1), F32), s((128, C), BF16), s((128, C), BF16), s((3, 2, C), F32), s((2, C), F32),
         s((2, C, 2 * C), BF16)],
    )(gaps, tok, cot, jnp.transpose(taps, (1, 0, 2)), gains, proj)
    tokens_grad, keep, send = call(
        body,
        "vvvvvvvv",
        [s((128, C), BF16), s((ACT, 3 * C), BF16), s((ACT, 3 * C), BF16)],
        [v((384, C), F32), v((384, 1), F32), v((320, C), F32), v((320, C), BF16), v((320, 2 * C), F32),
         v((320, C), F32), v((320, C), F32), v((320, 1), F32), v((256, C), F32), v((256, C), BF16),
         v((256, 2 * C), F32), v((256, 2 * C), BF16), v((256, C), F32), v((128, C), F32),
         v((192, 2 * C), BF16), v((192, C), F32), v((2, ACT, 3 * C), BF16)],
    )(near_args[0], prev, nxt, *near_args[1:])
    recv = lax.ppermute(send, "c", [(0, 1), (1, 0)])
    part = call(terms, "vv", s((8, 528, 128), BF16))(keep, recv)
    part = lax.all_to_all(part, NEAR, 0, 0, tiled=True)
    part = call(first_sum, "v", s((32, 32, 128), BF16))(part)
    part = lax.all_to_all(part, FAR, 0, 0, tiled=True)
    part = call(second_sum, "v", s((32, 128), F32))(part)
    part = lax.all_gather(part, HAP, axis=0)
    projection_grad, taps_grad, gains_grad = call(
        place, "v", [s((2, 4, 1024), F32), s((3, 2, C), F32), s((2, C), F32)]
    )(part)
    return tokens_grad[None], projection_grad, jnp.transpose(taps_grad, (1, 0, 2)), gains_grad


def solution(mesh):
    fine = Mesh(mesh.devices.reshape(8, 4, 4, 2, 2), ("z", "x", "yh", "yl", "c"))
    return jax.shard_map(
        shards,
        mesh=fine,
        in_specs=(P(HAP, SEQ, None), P(HAP, SEQ, None), P(SEQ, None), P(), P(), P()),
        out_specs=(P(HAP, SEQ, None), P(None, SEQ, None), P(), P()),
        check_vma=False,
    )
```

```python
import jax
import jax.numpy as jnp
from jax import lax
from jax.experimental import pallas as pl
from jax.experimental.pallas import tpu as pltpu
from jax.sharding import Mesh
from jax.sharding import PartitionSpec as P

C = 512
DIL = 32
EPS = 1e-06
F32 = jnp.float32
BF16 = jnp.bfloat16
NEAR = ("x", "yl")
FAR = ("z", "yh")
SEQ = ("z", "x", "yh")
HAP = ("yl", "c")
G0 = 0.7978845608028654
G1 = 0.044715
MARK = 64.0
ACT = 144


def gelu_and_slope(x, with_slope=True):
    x2 = x * x
    cdf = 0.5 + 0.5 * jnp.tanh(x * (G0 + (G0 * G1) * x2))
    hid = x * cdf
    if not with_slope:
        return hid, None
    return hid, cdf + hid * (1.0 - cdf) * (2.0 * G0 + (6.0 * G0 * G1) * x2)


def sigmoid(x):
    return 0.5 + 0.5 * jnp.tanh(0.5 * x)


def dot(a, b, dims):
    return lax.dot_general(a, b, (dims, ((), ())), preferred_element_type=F32)


def fold8(v):
    return jnp.sum(v.reshape(v.shape[0] // 8, 8, v.shape[1]), axis=0)


def hi_lo(v):
    hi = v.astype(BF16)
    lo = (v - hi.astype(F32)).astype(BF16)
    return hi, lo


def pack(gaps, tok, cot, up, down):
    at = lax.broadcasted_iota(jnp.int32, (128, 1), 0)
    inside = (at >= gaps[0, 0]) & (at < gaps[0, 1])
    marked = jnp.where(inside, MARK, tok[...].astype(F32)).astype(BF16)
    up[0:128, :] = marked
    down[0:128, :] = marked
    up[128:192, :] = cot[64:128, :]
    down[128:192, :] = cot[0:64, :]


def warm(gaps, tok, cot, taps, gains, proj, valid, tok_out, cot_out, taps_out, gains_out, proj_out):
    at = lax.broadcasted_iota(jnp.int32, (128, 1), 0)
    valid[...] = jnp.where((at >= gaps[0, 0]) & (at < gaps[0, 1]), 0.0, 1.0)
    for a, b in ((tok, tok_out), (cot, cot_out), (taps, taps_out), (gains, gains_out), (proj, proj_out)):
        b[...] = a[...]


def body(own_valid, prev, nxt, tok, cot, taps, gains, proj, out, keep, send,
         n0, i0, g0, h0, ab0, x1, n1, i1, g1, h1, po1, dp1, dh1, gr1, dp0, dh0, act):
    core = lax.axis_index("c")
    place_in_seq = sum(lax.axis_index(a) for a in SEQ)
    inner = (place_in_seq > 0, None, place_in_seq < 13)

    def rows(base):
        ref, at = ((prev, base), (tok, base - 128), (nxt, base - 256))[base // 128]
        return ref[at:at + DIL, :].astype(F32)

    def cot_rows(base):
        if base < 128:
            return prev[128 + base - 64:128 + base - 32, :].astype(F32)
        if base < 256:
            return cot[base - 128:base - 96, :].astype(F32)
        return nxt[128 + base - 256:128 + base - 224, :].astype(F32)

    valid_of = []
    for chunk in range(12):
        if 4 <= chunk < 8:
            valid_of.append(own_valid[DIL * (chunk - 4):DIL * (chunk - 3), :])
        else:
            ref = prev if chunk < 4 else nxt
            lead = ref[DIL * (chunk % 4):DIL * (chunk % 4) + DIL, 0:128].astype(F32)[:, 0:1]
            valid_of.append(jnp.where(lead < 0.5 * MARK, jnp.where(inner[chunk // 4], 1.0, 0.0), 0.0))

    def norm(v, valid, gain):
        inv = lax.rsqrt(jnp.sum(v * v, axis=-1, keepdims=True) * (1.0 / C) + EPS)
        return inv, v * (inv * valid) * gain

    def tap(layer, k):
        return taps[k, layer:layer + 1, :]

    def conv(ref, at, layer):
        return (tap(layer, 0) * ref[at - DIL:at, :] + tap(layer, 1) * ref[at:at + DIL, :]
                + tap(layer, 2) * ref[at + DIL:at + 2 * DIL, :])

    for c in range(12):
        inv, normed = norm(rows(c * DIL), valid_of[c], gains[0:1, :])
        if 4 <= c < 8:
            i0[c * DIL:(c + 1) * DIL, :] = inv
        n0[c * DIL:(c + 1) * DIL, :] = normed
    for c in range(1, 11):
        hid, slope = gelu_and_slope(conv(n0, c * DIL, 0), 3 <= c < 9)
        h0[(c - 1) * DIL:c * DIL, :] = hid.astype(BF16)
        if 3 <= c < 9:
            g0[(c - 1) * DIL:c * DIL, :] = slope
    ab0[...] = dot(h0[...], proj[0], ((1,), (0,)))
    for c in range(1, 11):
        at = slice((c - 1) * DIL, c * DIL)
        first = ab0[at, 0:C]
        gate = sigmoid(ab0[at, C:2 * C])
        both = first * gate
        nx = (rows(c * DIL) + valid_of[c] * both).astype(BF16).astype(F32)
        inv, normed = norm(nx, valid_of[c], gains[1:2, :])
        if 3 <= c < 9:
            ab0[at, 0:C] = gate
            ab0[at, C:2 * C] = both * (1.0 - gate)
            x1[at, :] = nx
            i1[at, :] = inv
        n1[at, :] = normed
    for c in range(2, 10):
        hid, slope = gelu_and_slope(conv(n1, (c - 1) * DIL, 1))
        h1[(c - 2) * DIL:(c - 1) * DIL, :] = hid.astype(BF16)
        g1[(c - 2) * DIL:(c - 1) * DIL, :] = slope
    po1[...] = dot(h1[...], proj[1], ((1,), (0,)))
    for c in range(2, 10):
        at = slice((c - 2) * DIL, (c - 1) * DIL)
        first = po1[at, 0:C]
        gate = sigmoid(po1[at, C:2 * C])
        bg = valid_of[c] * cot_rows(c * DIL) * gate
        dp1[at, 0:C] = bg.astype(BF16)
        dp1[at, C:2 * C] = (bg * first * (1.0 - gate)).astype(BF16)
    dh1[...] = dot(dp1[...], proj[1], ((1,), (1,))) * g1[...]

    def back(dref, c_off, layer, c, sref_rows, inv, valid, gain):
        at = c_off
        dn = (tap(layer, 0) * dref[at + DIL:at + 2 * DIL, :] + tap(layer, 1) * dref[at:at + DIL, :]
              + tap(layer, 2) * dref[at - DIL:at, :])
        dq = dn * valid
        si = sref_rows * inv
        qs = dq * si
        dt = dq * gain
        m = jnp.sum(qs * gain, axis=-1, keepdims=True) * (1.0 / C)
        return inv * (dt - si * m), qs

    def small_rows(parts):
        return [jnp.sum(p, axis=0, keepdims=True) for p in parts]

    acc = [jnp.zeros((8, C), F32) for _ in range(4)]
    for c in range(3, 9):
        at1 = slice((c - 1) * DIL, c * DIL)
        delta, qs = back(dh1, (c - 2) * DIL, 1, c, x1[at1, :], i1[at1, :], valid_of[c], gains[1:2, :])
        grad = cot_rows(c * DIL) + delta
        branch = valid_of[c] * grad
        to = slice((c - 3) * DIL, (c - 2) * DIL)
        dp0[to, 0:C] = (branch * ab0[at1, 0:C]).astype(BF16)
        dp0[to, C:2 * C] = (branch * ab0[at1, C:2 * C]).astype(BF16)
        if 4 <= c < 8:
            gr1[(c - 4) * DIL:(c - 3) * DIL, :] = grad
            d = dh1[(c - 2) * DIL:(c - 1) * DIL, :]
            for k in range(3):
                acc[k] += fold8(d * n1[(c - 2 + k) * DIL:(c - 1 + k) * DIL, :])
            acc[3] += fold8(qs)

    def put(layer, hid, dpr, parts):
        act[layer, 0:128, 0:C] = hid
        act[layer, 0:128, C:3 * C] = dpr
        four = jnp.concatenate(small_rows(parts) + [jnp.zeros((12, C), F32)], axis=0)
        hi, lo = hi_lo(four)
        act[layer, 128:ACT, 0:C] = hi
        act[layer, 128:ACT, C:2 * C] = lo
        act[layer, 128:ACT, 2 * C:3 * C] = jnp.zeros((16, C), BF16)

    put(1, h1[64:192, :], dp1[64:192, :], acc)

    dh0[...] = dot(dp0[...], proj[0], ((1,), (1,))) * g0[64:256, :]
    acc = [jnp.zeros((8, C), F32) for _ in range(4)]
    for c in range(4, 8):
        delta, qs = back(dh0, (c - 3) * DIL, 0, c, rows(c * DIL), i0[c * DIL:(c + 1) * DIL, :],
                         valid_of[c], gains[0:1, :])
        at = slice((c - 4) * DIL, (c - 3) * DIL)
        out[at, :] = (gr1[at, :] + delta).astype(BF16)
        d = dh0[(c - 3) * DIL:(c - 2) * DIL, :]
        for k in range(3):
            acc[k] += fold8(d * n0[(c - 1 + k) * DIL:(c + k) * DIL, :])
        acc[3] += fold8(qs)
    put(0, h0[96:224, :], dp0[32:160, :], acc)
    keep[...] = act[core]
    send[...] = act[1 - core]


def own_terms(keep, pick, mine):
    q = lax.broadcasted_iota(jnp.int32, (C, 1), 0)
    ch = ((q >> 3) & 7) << 6 | ((q >> 7) & 3) << 4 | ((q >> 1) & 3) << 2 | ((q >> 6) & 1) << 1 | (q & 1)
    pick[...] = (ch == lax.broadcasted_iota(jnp.int32, (C, C), 1)).astype(F32).astype(BF16)
    ha = dot(pick[...], keep[0:128, 0:C], ((1,), (1,))).astype(BF16)
    mine[...] = dot(ha, keep[0:128, C:3 * C], ((1,), (0,)))


def terms(keep, recv, pick, mine, out):
    hb = dot(pick[...], recv[0:128, 0:C], ((1,), (1,))).astype(BF16)
    for j in range(8):
        cols = slice(j * 128, (j + 1) * 128)
        t = mine[:, cols] + dot(hb, recv[0:128, C + j * 128:C + (j + 1) * 128], ((1,), (0,)))
        out[:, j * 64:(j + 1) * 64, :] = t.astype(BF16).reshape(8, 64, 128)
    small = (keep[128:ACT, 0:C].astype(F32) + keep[128:ACT, C:2 * C].astype(F32)
             + recv[128:ACT, 0:C].astype(F32) + recv[128:ACT, C:2 * C].astype(F32))
    tile = jnp.concatenate(
        [small[r:r + 1, 128 * q:128 * (q + 1)] for r in range(4) for q in range(4)], axis=0).astype(BF16)
    for g in range(8):
        out[g, 512:528, :] = tile


def first_sum(recv, out):
    total = recv[0].astype(F32)
    for i in range(1, 8):
        total += recv[i].astype(F32)
    p = lax.broadcasted_iota(jnp.int32, (C, 1), 0)
    src = ((p >> 1) & 7) << 6 | (p >> 4) << 1 | (p & 1)
    pick = (src == lax.broadcasted_iota(jnp.int32, (C, C), 1)).astype(F32).astype(BF16)
    moved = dot(pick, total[0:512, :].astype(BF16), ((1,), (0,))).astype(BF16)
    out[:, 0:16, :] = moved.reshape(32, 16, 128)
    tile = total[512:528, :].astype(BF16)
    for d in range(32):
        out[d, 16:32, :] = tile


def second_sum(recv, out):
    total = recv[0].astype(F32)
    for i in range(1, 32):
        total += recv[i].astype(F32)
    out[...] = total


def place(recv, proj, taps, gains):
    for c in range(2):
        for y in range(2):
            for j in range(8):
                proj[c, 2 * y:2 * y + 2, j * 128:(j + 1) * 128] = recv[y * 2 + c, 2 * j:2 * j + 2, :]
        for r in range(4):
            for q in range(4):
                row = recv[c, 16 + r * 4 + q:17 + r * 4 + q, :]
                if r < 3:
                    taps[r, c:c + 1, q * 128:(q + 1) * 128] = row
                else:
                    gains[c:c + 1, q * 128:(q + 1) * 128] = row


def call(kernel, ins, outs, scratch=(), mib=48):
    single = not isinstance(outs, (list, tuple))
    vmem = pl.BlockSpec(memory_space=pltpu.VMEM)
    return pl.pallas_call(
        kernel,
        out_shape=outs,
        in_specs=[pl.BlockSpec(memory_space={"v": pltpu.VMEM, "s": pltpu.SMEM, "a": pl.ANY}[m]) for m in ins],
        out_specs=vmem if single else [vmem] * len(outs),
        scratch_shapes=list(scratch),
        compiler_params=pltpu.CompilerParams(vmem_limit_bytes=int(mib * 1024 * 1024)),
    )


def main(*args):
    s = jax.ShapeDtypeStruct
    v = pltpu.VMEM
    return call(
        body,
        "vvvvvvvv",
        [s((128, C), BF16), s((ACT, 3 * C), BF16), s((ACT, 3 * C), BF16)],
        [v((384, C), F32), v((384, 1), F32), v((320, C), F32), v((320, C), BF16), v((320, 2 * C), F32),
         v((320, C), F32), v((320, C), F32), v((320, 1), F32), v((256, C), F32), v((256, C), BF16),
         v((256, 2 * C), F32), v((256, 2 * C), BF16), v((256, C), F32), v((128, C), F32),
         v((192, 2 * C), BF16), v((192, C), F32), v((2, ACT, 3 * C), BF16)],
    )(*args)


def shards(tokens, cotangent, gaps, taps, gains, proj):
    tok, cot = tokens[0], cotangent[0]
    n = 128
    s = jax.ShapeDtypeStruct
    far = [pltpu.with_memory_space_constraint(a, pltpu.HBM) for a in (gaps, tok, cot)]
    up, down = call(pack, "svv", [s((192, C), BF16), s((192, C), BF16)], mib=48)(*far)
    prev = lax.ppermute(up, SEQ, [(i, i + 1) for i in range(n - 1)])
    nxt = lax.ppermute(down, SEQ, [(i + 1, i) for i in range(n - 1)])
    here = [jnp.transpose(taps, (1, 0, 2)), gains, proj]
    here = far + [pltpu.with_memory_space_constraint(a, pltpu.HBM) for a in here]
    near_args = call(
        warm,
        "svvvvv",
        [s((128, 1), F32), s((128, C), BF16), s((128, C), BF16), s((3, 2, C), F32), s((2, C), F32),
         s((2, C, 2 * C), BF16)],
    )(*here)
    tokens_grad, keep, send = main(near_args[0], prev, nxt, *near_args[1:])
    recv = lax.ppermute(send, "c", [(0, 1), (1, 0)])
    pick, mine = call(own_terms, "v", [s((C, C), BF16), s((C, 2 * C), F32)])(keep)
    part = call(terms, "vvvv", s((8, 528, 128), BF16))(keep, recv, pick, mine)
    part = lax.all_to_all(part, NEAR, 0, 0, tiled=True)
    part = call(first_sum, "v", s((32, 32, 128), BF16))(part)
    part = lax.all_to_all(part, FAR, 0, 0, tiled=True)
    part = call(second_sum, "v", s((32, 128), F32))(part)
    part = lax.all_gather(part, HAP, axis=0)
    projection_grad, taps_grad, gains_grad = call(
        place, "v", [s((2, 4, 1024), F32), s((3, 2, C), F32), s((2, C), F32)]
    )(part)
    return tokens_grad[None], projection_grad, jnp.transpose(taps_grad, (1, 0, 2)), gains_grad


def solution(mesh):
    fine = Mesh(mesh.devices.reshape(8, 4, 4, 2, 2), ("z", "x", "yh", "yl", "c"))
    return jax.shard_map(
        shards,
        mesh=fine,
        in_specs=(P(HAP, SEQ, None), P(HAP, SEQ, None), P(SEQ, None), P(), P(), P()),
        out_specs=(P(HAP, SEQ, None), P(None, SEQ, None), P(), P()),
        check_vma=False,
    )
```

```python
import jax
import jax.numpy as jnp
from jax import lax
from jax.experimental import pallas as pl
from jax.experimental.pallas import tpu as pltpu
from jax.sharding import Mesh
from jax.sharding import PartitionSpec as P

C = 512
DIL = 32
EPS = 1e-06
F32 = jnp.float32
BF16 = jnp.bfloat16
NEAR = ("zl", "x", "yl")
FAR = ("zh", "yh")
SEQ = ("zh", "zl", "x", "yh")
HAP = ("yl", "c")
G0 = 0.7978845608028654
G1 = 0.044715
MARK = 64.0
ACT = 144


def gelu_and_slope(x, with_slope=True):
    x2 = x * x
    cdf = 0.5 + 0.5 * jnp.tanh(x * (G0 + (G0 * G1) * x2))
    hid = x * cdf
    if not with_slope:
        return hid, None
    return hid, cdf + hid * (1.0 - cdf) * (2.0 * G0 + (6.0 * G0 * G1) * x2)


def sigmoid(x):
    return 0.5 + 0.5 * jnp.tanh(0.5 * x)


def dot(a, b, dims):
    return lax.dot_general(a, b, (dims, ((), ())), preferred_element_type=F32)


def fold8(v):
    return jnp.sum(v.reshape(v.shape[0] // 8, 8, v.shape[1]), axis=0)


def hi_lo(v):
    hi = v.astype(BF16)
    lo = (v - hi.astype(F32)).astype(BF16)
    return hi, lo


def pack(gaps, tok, cot, up, down):
    at = lax.broadcasted_iota(jnp.int32, (128, 1), 0)
    inside = (at >= gaps[0, 0]) & (at < gaps[0, 1])
    marked = jnp.where(inside, MARK, tok[...].astype(F32)).astype(BF16)
    up[0:128, :] = marked
    down[0:128, :] = marked
    up[128:192, :] = cot[64:128, :]
    down[128:192, :] = cot[0:64, :]


def warm(gaps, tok, cot, taps, gains, proj, valid, tok_out, cot_out, taps_out, gains_out, proj_out):
    at = lax.broadcasted_iota(jnp.int32, (128, 1), 0)
    valid[...] = jnp.where((at >= gaps[0, 0]) & (at < gaps[0, 1]), 0.0, 1.0)
    for a, b in ((tok, tok_out), (cot, cot_out), (taps, taps_out), (gains, gains_out), (proj, proj_out)):
        b[...] = a[...]


def body(own_valid, prev, nxt, tok, cot, taps, gains, proj, out, keep, send,
         n0, i0, g0, h0, ab0, x1, n1, i1, g1, h1, po1, dp1, dh1, gr1, dp0, dh0, act):
    core = lax.axis_index("c")
    place_in_seq = sum(lax.axis_index(a) for a in SEQ)
    inner = (place_in_seq > 0, None, place_in_seq < 10)

    def rows(base):
        ref, at = ((prev, base), (tok, base - 128), (nxt, base - 256))[base // 128]
        return ref[at:at + DIL, :].astype(F32)

    def cot_rows(base):
        if base < 128:
            return prev[128 + base - 64:128 + base - 32, :].astype(F32)
        if base < 256:
            return cot[base - 128:base - 96, :].astype(F32)
        return nxt[128 + base - 256:128 + base - 224, :].astype(F32)

    valid_of = []
    for chunk in range(12):
        if 4 <= chunk < 8:
            valid_of.append(own_valid[DIL * (chunk - 4):DIL * (chunk - 3), :])
        else:
            ref = prev if chunk < 4 else nxt
            lead = ref[DIL * (chunk % 4):DIL * (chunk % 4) + DIL, 0:128].astype(F32)[:, 0:1]
            valid_of.append(jnp.where(lead < 0.5 * MARK, jnp.where(inner[chunk // 4], 1.0, 0.0), 0.0))

    def norm(v, valid, gain):
        inv = lax.rsqrt(jnp.sum(v * v, axis=-1, keepdims=True) * (1.0 / C) + EPS)
        return inv, v * (inv * valid) * gain

    def tap(layer, k):
        return taps[k, layer:layer + 1, :]

    def conv(ref, at, layer):
        return (tap(layer, 0) * ref[at - DIL:at, :] + tap(layer, 1) * ref[at:at + DIL, :]
                + tap(layer, 2) * ref[at + DIL:at + 2 * DIL, :])

    for c in range(12):
        inv, normed = norm(rows(c * DIL), valid_of[c], gains[0:1, :])
        if 4 <= c < 8:
            i0[c * DIL:(c + 1) * DIL, :] = inv
        n0[c * DIL:(c + 1) * DIL, :] = normed
    for c in range(1, 11):
        hid, slope = gelu_and_slope(conv(n0, c * DIL, 0), 3 <= c < 9)
        h0[(c - 1) * DIL:c * DIL, :] = hid.astype(BF16)
        if 3 <= c < 9:
            g0[(c - 1) * DIL:c * DIL, :] = slope
    ab0[...] = dot(h0[...], proj[0], ((1,), (0,)))
    for c in range(1, 11):
        at = slice((c - 1) * DIL, c * DIL)
        first = ab0[at, 0:C]
        gate = sigmoid(ab0[at, C:2 * C])
        both = first * gate
        nx = (rows(c * DIL) + valid_of[c] * both).astype(BF16).astype(F32)
        inv, normed = norm(nx, valid_of[c], gains[1:2, :])
        if 3 <= c < 9:
            ab0[at, 0:C] = gate
            ab0[at, C:2 * C] = both * (1.0 - gate)
            x1[at, :] = nx
            i1[at, :] = inv
        n1[at, :] = normed
    for c in range(2, 10):
        hid, slope = gelu_and_slope(conv(n1, (c - 1) * DIL, 1))
        h1[(c - 2) * DIL:(c - 1) * DIL, :] = hid.astype(BF16)
        g1[(c - 2) * DIL:(c - 1) * DIL, :] = slope
    po1[...] = dot(h1[...], proj[1], ((1,), (0,)))
    for c in range(2, 10):
        at = slice((c - 2) * DIL, (c - 1) * DIL)
        first = po1[at, 0:C]
        gate = sigmoid(po1[at, C:2 * C])
        bg = valid_of[c] * cot_rows(c * DIL) * gate
        dp1[at, 0:C] = bg.astype(BF16)
        dp1[at, C:2 * C] = (bg * first * (1.0 - gate)).astype(BF16)
    dh1[...] = dot(dp1[...], proj[1], ((1,), (1,))) * g1[...]

    def back(dref, c_off, layer, c, sref_rows, inv, valid, gain):
        at = c_off
        dn = (tap(layer, 0) * dref[at + DIL:at + 2 * DIL, :] + tap(layer, 1) * dref[at:at + DIL, :]
              + tap(layer, 2) * dref[at - DIL:at, :])
        dq = dn * valid
        si = sref_rows * inv
        qs = dq * si
        dt = dq * gain
        m = jnp.sum(qs * gain, axis=-1, keepdims=True) * (1.0 / C)
        return inv * (dt - si * m), qs

    def small_rows(parts):
        return [jnp.sum(p, axis=0, keepdims=True) for p in parts]

    acc = [jnp.zeros((8, C), F32) for _ in range(4)]
    for c in range(3, 9):
        at1 = slice((c - 1) * DIL, c * DIL)
        delta, qs = back(dh1, (c - 2) * DIL, 1, c, x1[at1, :], i1[at1, :], valid_of[c], gains[1:2, :])
        grad = cot_rows(c * DIL) + delta
        branch = valid_of[c] * grad
        to = slice((c - 3) * DIL, (c - 2) * DIL)
        dp0[to, 0:C] = (branch * ab0[at1, 0:C]).astype(BF16)
        dp0[to, C:2 * C] = (branch * ab0[at1, C:2 * C]).astype(BF16)
        if 4 <= c < 8:
            gr1[(c - 4) * DIL:(c - 3) * DIL, :] = grad
            d = dh1[(c - 2) * DIL:(c - 1) * DIL, :]
            for k in range(3):
                acc[k] += fold8(d * n1[(c - 2 + k) * DIL:(c - 1 + k) * DIL, :])
            acc[3] += fold8(qs)

    def put(layer, hid, dpr, parts):
        act[layer, 0:128, 0:C] = hid
        act[layer, 0:128, C:3 * C] = dpr
        four = jnp.concatenate(small_rows(parts) + [jnp.zeros((12, C), F32)], axis=0)
        hi, lo = hi_lo(four)
        act[layer, 128:ACT, 0:C] = hi
        act[layer, 128:ACT, C:2 * C] = lo
        act[layer, 128:ACT, 2 * C:3 * C] = jnp.zeros((16, C), BF16)

    put(1, h1[64:192, :], dp1[64:192, :], acc)

    dh0[...] = dot(dp0[...], proj[0], ((1,), (1,))) * g0[64:256, :]
    acc = [jnp.zeros((8, C), F32) for _ in range(4)]
    for c in range(4, 8):
        delta, qs = back(dh0, (c - 3) * DIL, 0, c, rows(c * DIL), i0[c * DIL:(c + 1) * DIL, :],
                         valid_of[c], gains[0:1, :])
        at = slice((c - 4) * DIL, (c - 3) * DIL)
        out[at, :] = (gr1[at, :] + delta).astype(BF16)
        d = dh0[(c - 3) * DIL:(c - 2) * DIL, :]
        for k in range(3):
            acc[k] += fold8(d * n0[(c - 1 + k) * DIL:(c + k) * DIL, :])
        acc[3] += fold8(qs)
    put(0, h0[96:224, :], dp0[32:160, :], acc)
    keep[...] = act[core]
    send[...] = act[1 - core]


def own_terms(keep, pick, mine):
    q = lax.broadcasted_iota(jnp.int32, (C, 1), 0)
    ch = (((q >> 3) & 3) << 7 | ((q >> 8) & 1) << 6 | ((q >> 6) & 3) << 4 | ((q >> 1) & 3) << 2
          | ((q >> 5) & 1) << 1 | (q & 1))
    pick[...] = (ch == lax.broadcasted_iota(jnp.int32, (C, C), 1)).astype(F32).astype(BF16)
    ha = dot(pick[...], keep[0:128, 0:C], ((1,), (1,))).astype(BF16)
    mine[...] = dot(ha, keep[0:128, C:3 * C], ((1,), (0,)))


def terms(keep, recv, pick, mine, out):
    hb = dot(pick[...], recv[0:128, 0:C], ((1,), (1,))).astype(BF16)
    for j in range(8):
        cols = slice(j * 128, (j + 1) * 128)
        t = mine[:, cols] + dot(hb, recv[0:128, C + j * 128:C + (j + 1) * 128], ((1,), (0,)))
        out[:, j * 32:(j + 1) * 32, :] = t.astype(BF16).reshape(16, 32, 128)
    small = (keep[128:ACT, 0:C].astype(F32) + keep[128:ACT, C:2 * C].astype(F32)
             + recv[128:ACT, 0:C].astype(F32) + recv[128:ACT, C:2 * C].astype(F32))
    tile = jnp.concatenate(
        [small[r:r + 1, 128 * q:128 * (q + 1)] for r in range(4) for q in range(4)], axis=0).astype(BF16)
    for g in range(16):
        out[g, 256:272, :] = tile


def first_sum(recv, out):
    total = recv[0].astype(F32)
    for i in range(1, 16):
        total += recv[i].astype(F32)
    p = lax.broadcasted_iota(jnp.int32, (256, 1), 0)
    src = ((p >> 1) & 7) << 5 | (p >> 4) << 1 | (p & 1)
    pick = (src == lax.broadcasted_iota(jnp.int32, (256, 256), 1)).astype(F32).astype(BF16)
    moved = dot(pick, total[0:256, :].astype(BF16), ((1,), (0,))).astype(BF16)
    out[:, 0:16, :] = moved.reshape(16, 16, 128)
    tile = total[256:272, :].astype(BF16)
    for d in range(16):
        out[d, 16:32, :] = tile


def second_sum(recv, out):
    total = recv[0].astype(F32)
    for i in range(1, 16):
        total += recv[i].astype(F32)
    out[...] = total


def place(recv, proj, taps, gains):
    for c in range(2):
        for y in range(2):
            for j in range(8):
                proj[c, 2 * y:2 * y + 2, j * 128:(j + 1) * 128] = recv[y * 2 + c, 2 * j:2 * j + 2, :]
        for r in range(4):
            for q in range(4):
                row = recv[c, 16 + r * 4 + q:17 + r * 4 + q, :]
                if r < 3:
                    taps[r, c:c + 1, q * 128:(q + 1) * 128] = row
                else:
                    gains[c:c + 1, q * 128:(q + 1) * 128] = row


def call(kernel, ins, outs, scratch=(), mib=48):
    single = not isinstance(outs, (list, tuple))
    vmem = pl.BlockSpec(memory_space=pltpu.VMEM)
    return pl.pallas_call(
        kernel,
        out_shape=outs,
        in_specs=[pl.BlockSpec(memory_space={"v": pltpu.VMEM, "s": pltpu.SMEM, "a": pl.ANY}[m]) for m in ins],
        out_specs=vmem if single else [vmem] * len(outs),
        scratch_shapes=list(scratch),
        compiler_params=pltpu.CompilerParams(vmem_limit_bytes=int(mib * 1024 * 1024)),
    )


def main(*args):
    s = jax.ShapeDtypeStruct
    v = pltpu.VMEM
    return call(
        body,
        "vvvvvvvv",
        [s((128, C), BF16), s((ACT, 3 * C), BF16), s((ACT, 3 * C), BF16)],
        [v((384, C), F32), v((384, 1), F32), v((320, C), F32), v((320, C), BF16), v((320, 2 * C), F32),
         v((320, C), F32), v((320, C), F32), v((320, 1), F32), v((256, C), F32), v((256, C), BF16),
         v((256, 2 * C), F32), v((256, 2 * C), BF16), v((256, C), F32), v((128, C), F32),
         v((192, 2 * C), BF16), v((192, C), F32), v((2, ACT, 3 * C), BF16)],
    )(*args)


def shards(tokens, cotangent, gaps, taps, gains, proj):
    tok, cot = tokens[0], cotangent[0]
    n = 128
    s = jax.ShapeDtypeStruct
    far = [pltpu.with_memory_space_constraint(a, pltpu.HBM) for a in (gaps, tok, cot)]
    up, down = call(pack, "svv", [s((192, C), BF16), s((192, C), BF16)], mib=48)(*far)
    prev = lax.ppermute(up, SEQ, [(i, i + 1) for i in range(n - 1)])
    nxt = lax.ppermute(down, SEQ, [(i + 1, i) for i in range(n - 1)])
    here = [jnp.transpose(taps, (1, 0, 2)), gains, proj]
    here = far + [pltpu.with_memory_space_constraint(a, pltpu.HBM) for a in here]
    near_args = call(
        warm,
        "svvvvv",
        [s((128, 1), F32), s((128, C), BF16), s((128, C), BF16), s((3, 2, C), F32), s((2, C), F32),
         s((2, C, 2 * C), BF16)],
    )(*here)
    tokens_grad, keep, send = main(near_args[0], prev, nxt, *near_args[1:])
    recv = lax.ppermute(send, "c", [(0, 1), (1, 0)])
    pick, mine = call(own_terms, "v", [s((C, C), BF16), s((C, 2 * C), F32)])(keep)
    part = call(terms, "vvvv", s((16, 272, 128), BF16))(keep, recv, pick, mine)
    part = lax.all_to_all(part, NEAR, 0, 0, tiled=True)
    part = call(first_sum, "v", s((16, 32, 128), BF16))(part)
    part = lax.all_to_all(part, FAR, 0, 0, tiled=True)
    part = call(second_sum, "v", s((32, 128), F32))(part)
    part = lax.all_gather(part, HAP, axis=0)
    projection_grad, taps_grad, gains_grad = call(
        place, "v", [s((2, 4, 1024), F32), s((3, 2, C), F32), s((2, C), F32)]
    )(part)
    return tokens_grad[None], projection_grad, jnp.transpose(taps_grad, (1, 0, 2)), gains_grad


def solution(mesh):
    fine = Mesh(mesh.devices.reshape(4, 2, 4, 4, 2, 2), ("zh", "zl", "x", "yh", "yl", "c"))
    return jax.shard_map(
        shards,
        mesh=fine,
        in_specs=(P(HAP, SEQ, None), P(HAP, SEQ, None), P(SEQ, None), P(), P(), P()),
        out_specs=(P(HAP, SEQ, None), P(None, SEQ, None), P(), P()),
        check_vma=False,
    )
```

```python
import jax
import jax.numpy as jnp
from jax import lax
from jax.experimental import pallas as pl
from jax.experimental.pallas import tpu as pltpu
from jax.sharding import Mesh
from jax.sharding import PartitionSpec as P

C = 512
DIL = 32
EPS = 1e-06
F32 = jnp.float32
BF16 = jnp.bfloat16
ALL = ("z", "x", "yh", "yl", "c")
SEQ = ("z", "x", "yh")
HAP = ("yl", "c")
G0 = 0.7978845608028654
G1 = 0.044715
MARK = 64.0
ACT = 144


def gelu_and_slope(x, with_slope=True):
    x2 = x * x
    cdf = 0.5 + 0.5 * jnp.tanh(x * (G0 + (G0 * G1) * x2))
    hid = x * cdf
    if not with_slope:
        return hid, None
    return hid, cdf + hid * (1.0 - cdf) * (2.0 * G0 + (6.0 * G0 * G1) * x2)


def sigmoid(x):
    return 0.5 + 0.5 * jnp.tanh(0.5 * x)


def dot(a, b, dims):
    return lax.dot_general(a, b, (dims, ((), ())), preferred_element_type=F32)


def fold8(v):
    return jnp.sum(v.reshape(v.shape[0] // 8, 8, v.shape[1]), axis=0)


def hi_lo(v):
    hi = v.astype(BF16)
    lo = (v - hi.astype(F32)).astype(BF16)
    return hi, lo


def pack(gaps, tok, cot, up, down):
    at = lax.broadcasted_iota(jnp.int32, (128, 1), 0)
    inside = (at >= gaps[0, 0]) & (at < gaps[0, 1])
    marked = jnp.where(inside, MARK, tok[...].astype(F32)).astype(BF16)
    up[0:128, :] = marked
    down[0:128, :] = marked
    up[128:192, :] = cot[64:128, :]
    down[128:192, :] = cot[0:64, :]


def warm(gaps, tok, cot, taps, gains, proj, valid, tok_out, cot_out, taps_out, gains_out, proj_out):
    at = lax.broadcasted_iota(jnp.int32, (128, 1), 0)
    valid[...] = jnp.where((at >= gaps[0, 0]) & (at < gaps[0, 1]), 0.0, 1.0)
    for a, b in ((tok, tok_out), (cot, cot_out), (taps, taps_out), (gains, gains_out), (proj, proj_out)):
        b[...] = a[...]


def body(own_valid, prev, nxt, tok, cot, taps, gains, proj, out, keep, send,
         n0, i0, g0, h0, ab0, x1, n1, i1, g1, h1, po1, dp1, dh1, gr1, dp0, dh0, act):
    core = lax.axis_index("c")
    place_in_seq = sum(lax.axis_index(a) for a in SEQ)
    inner = (place_in_seq > 0, None, place_in_seq < 13)

    def rows(base):
        ref, at = ((prev, base), (tok, base - 128), (nxt, base - 256))[base // 128]
        return ref[at:at + DIL, :].astype(F32)

    def cot_rows(base):
        if base < 128:
            return prev[128 + base - 64:128 + base - 32, :].astype(F32)
        if base < 256:
            return cot[base - 128:base - 96, :].astype(F32)
        return nxt[128 + base - 256:128 + base - 224, :].astype(F32)

    valid_of = []
    for chunk in range(12):
        if 4 <= chunk < 8:
            valid_of.append(own_valid[DIL * (chunk - 4):DIL * (chunk - 3), :])
        else:
            ref = prev if chunk < 4 else nxt
            lead = ref[DIL * (chunk % 4):DIL * (chunk % 4) + DIL, 0:128].astype(F32)[:, 0:1]
            valid_of.append(jnp.where(lead < 0.5 * MARK, jnp.where(inner[chunk // 4], 1.0, 0.0), 0.0))

    def norm(v, valid, gain):
        inv = lax.rsqrt(jnp.sum(v * v, axis=-1, keepdims=True) * (1.0 / C) + EPS)
        return inv, v * (inv * valid) * gain

    def tap(layer, k):
        return taps[k, layer:layer + 1, :]

    def conv(ref, at, layer):
        return (tap(layer, 0) * ref[at - DIL:at, :] + tap(layer, 1) * ref[at:at + DIL, :]
                + tap(layer, 2) * ref[at + DIL:at + 2 * DIL, :])

    for c in range(12):
        inv, normed = norm(rows(c * DIL), valid_of[c], gains[0:1, :])
        if 4 <= c < 8:
            i0[c * DIL:(c + 1) * DIL, :] = inv
        n0[c * DIL:(c + 1) * DIL, :] = normed
    for c in range(1, 11):
        hid, slope = gelu_and_slope(conv(n0, c * DIL, 0), 3 <= c < 9)
        h0[(c - 1) * DIL:c * DIL, :] = hid.astype(BF16)
        if 3 <= c < 9:
            g0[(c - 1) * DIL:c * DIL, :] = slope
    ab0[...] = dot(h0[...], proj[0], ((1,), (0,)))
    for c in range(1, 11):
        at = slice((c - 1) * DIL, c * DIL)
        first = ab0[at, 0:C]
        gate = sigmoid(ab0[at, C:2 * C])
        both = first * gate
        nx = (rows(c * DIL) + valid_of[c] * both).astype(BF16).astype(F32)
        inv, normed = norm(nx, valid_of[c], gains[1:2, :])
        if 3 <= c < 9:
            ab0[at, 0:C] = gate
            ab0[at, C:2 * C] = both * (1.0 - gate)
            x1[at, :] = nx
            i1[at, :] = inv
        n1[at, :] = normed
    for c in range(2, 10):
        hid, slope = gelu_and_slope(conv(n1, (c - 1) * DIL, 1))
        h1[(c - 2) * DIL:(c - 1) * DIL, :] = hid.astype(BF16)
        g1[(c - 2) * DIL:(c - 1) * DIL, :] = slope
    po1[...] = dot(h1[...], proj[1], ((1,), (0,)))
    for c in range(2, 10):
        at = slice((c - 2) * DIL, (c - 1) * DIL)
        first = po1[at, 0:C]
        gate = sigmoid(po1[at, C:2 * C])
        bg = valid_of[c] * cot_rows(c * DIL) * gate
        dp1[at, 0:C] = bg.astype(BF16)
        dp1[at, C:2 * C] = (bg * first * (1.0 - gate)).astype(BF16)
    dh1[...] = dot(dp1[...], proj[1], ((1,), (1,))) * g1[...]

    def back(dref, c_off, layer, c, sref_rows, inv, valid, gain):
        at = c_off
        dn = (tap(layer, 0) * dref[at + DIL:at + 2 * DIL, :] + tap(layer, 1) * dref[at:at + DIL, :]
              + tap(layer, 2) * dref[at - DIL:at, :])
        dq = dn * valid
        si = sref_rows * inv
        qs = dq * si
        dt = dq * gain
        m = jnp.sum(qs * gain, axis=-1, keepdims=True) * (1.0 / C)
        return inv * (dt - si * m), qs

    def small_rows(parts):
        return [jnp.sum(p, axis=0, keepdims=True) for p in parts]

    acc = [jnp.zeros((8, C), F32) for _ in range(4)]
    for c in range(3, 9):
        at1 = slice((c - 1) * DIL, c * DIL)
        delta, qs = back(dh1, (c - 2) * DIL, 1, c, x1[at1, :], i1[at1, :], valid_of[c], gains[1:2, :])
        grad = cot_rows(c * DIL) + delta
        branch = valid_of[c] * grad
        to = slice((c - 3) * DIL, (c - 2) * DIL)
        dp0[to, 0:C] = (branch * ab0[at1, 0:C]).astype(BF16)
        dp0[to, C:2 * C] = (branch * ab0[at1, C:2 * C]).astype(BF16)
        if 4 <= c < 8:
            gr1[(c - 4) * DIL:(c - 3) * DIL, :] = grad
            d = dh1[(c - 2) * DIL:(c - 1) * DIL, :]
            for k in range(3):
                acc[k] += fold8(d * n1[(c - 2 + k) * DIL:(c - 1 + k) * DIL, :])
            acc[3] += fold8(qs)

    def put(layer, hid, dpr, parts):
        act[layer, 0:128, 0:C] = hid
        act[layer, 0:128, C:3 * C] = dpr
        four = jnp.concatenate(small_rows(parts) + [jnp.zeros((12, C), F32)], axis=0)
        hi, lo = hi_lo(four)
        act[layer, 128:ACT, 0:C] = hi
        act[layer, 128:ACT, C:2 * C] = lo
        act[layer, 128:ACT, 2 * C:3 * C] = jnp.zeros((16, C), BF16)

    put(1, h1[64:192, :], dp1[64:192, :], acc)

    dh0[...] = dot(dp0[...], proj[0], ((1,), (1,))) * g0[64:256, :]
    acc = [jnp.zeros((8, C), F32) for _ in range(4)]
    for c in range(4, 8):
        delta, qs = back(dh0, (c - 3) * DIL, 0, c, rows(c * DIL), i0[c * DIL:(c + 1) * DIL, :],
                         valid_of[c], gains[0:1, :])
        at = slice((c - 4) * DIL, (c - 3) * DIL)
        out[at, :] = (gr1[at, :] + delta).astype(BF16)
        d = dh0[(c - 3) * DIL:(c - 2) * DIL, :]
        for k in range(3):
            acc[k] += fold8(d * n0[(c - 1 + k) * DIL:(c + k) * DIL, :])
        acc[3] += fold8(qs)
    put(0, h0[96:224, :], dp0[32:160, :], acc)
    keep[...] = act[core]
    send[...] = act[1 - core]


def device(near, far, core):
    z = ((far >> 3) * 2 + (near >> 2) + core) % 8
    x = ((far >> 2) % 2 * 2 + (near >> 1) % 2 + core) % 4
    y = (far % 4 * 2 + near % 2 + core) % 8
    return ((z * 4 + x) * 8 + y) * 2 + core


NEAR = [[device(n, f, c) for n in range(8)] for c in range(2) for f in range(32)]
FAR = [[device(n, f, c) for f in range(32)] for c in range(2) for n in range(8)]


def own_terms(keep, pick, mine):
    core = lax.axis_index("c")
    q = lax.broadcasted_iota(jnp.int32, (C, 1), 0)
    z = ((((q >> 5) & 1) << 2 | ((q >> 4) & 1) << 1 | ((q >> 8) & 1)) + core) & 7
    x = ((((q >> 3) & 1) << 1 | ((q >> 7) & 1)) + core) & 3
    y = ((((q >> 1) & 3) << 1 | ((q >> 6) & 1)) + core) & 7
    ch = z << 6 | x << 4 | y << 1 | (q & 1)
    pick[...] = (ch == lax.broadcasted_iota(jnp.int32, (C, C), 1)).astype(F32).astype(BF16)
    ha = dot(pick[...], keep[0:128, 0:C], ((1,), (1,))).astype(BF16)
    mine[...] = dot(ha, keep[0:128, C:3 * C], ((1,), (0,)))


def terms(keep, recv, pick, mine, out):
    hb = dot(pick[...], recv[0:128, 0:C], ((1,), (1,))).astype(BF16)
    for j in range(8):
        cols = slice(j * 128, (j + 1) * 128)
        t = mine[:, cols] + dot(hb, recv[0:128, C + j * 128:C + (j + 1) * 128], ((1,), (0,)))
        out[:, j * 64:(j + 1) * 64, :] = t.astype(BF16).reshape(8, 64, 128)
    small = (keep[128:ACT, 0:C].astype(F32) + keep[128:ACT, C:2 * C].astype(F32)
             + recv[128:ACT, 0:C].astype(F32) + recv[128:ACT, C:2 * C].astype(F32))
    tile = jnp.concatenate(
        [small[r:r + 1, 128 * q:128 * (q + 1)] for r in range(4) for q in range(4)], axis=0).astype(BF16)
    for g in range(8):
        out[g, 512:528, :] = tile


def first_sum(recv, out):
    total = recv[0].astype(F32)
    for i in range(1, 8):
        total += recv[i].astype(F32)
    p = lax.broadcasted_iota(jnp.int32, (C, 1), 0)
    src = ((p >> 1) & 7) << 6 | (p >> 4) << 1 | (p & 1)
    pick = (src == lax.broadcasted_iota(jnp.int32, (C, C), 1)).astype(F32).astype(BF16)
    moved = dot(pick, total[0:512, :].astype(BF16), ((1,), (0,))).astype(BF16)
    out[:, 0:16, :] = moved.reshape(32, 16, 128)
    tile = total[512:528, :].astype(BF16)
    for d in range(32):
        out[d, 16:32, :] = tile


def second_sum(recv, out):
    total = recv[0].astype(F32)
    for i in range(1, 32):
        total += recv[i].astype(F32)
    out[...] = total


def place(recv, proj, taps, gains):
    for c in range(2):
        for y in range(2):
            for j in range(8):
                proj[c, 2 * y:2 * y + 2, j * 128:(j + 1) * 128] = recv[y * 2 + c, 2 * j:2 * j + 2, :]
        for r in range(4):
            for q in range(4):
                row = recv[c, 16 + r * 4 + q:17 + r * 4 + q, :]
                if r < 3:
                    taps[r, c:c + 1, q * 128:(q + 1) * 128] = row
                else:
                    gains[c:c + 1, q * 128:(q + 1) * 128] = row


def call(kernel, ins, outs, scratch=(), mib=48):
    single = not isinstance(outs, (list, tuple))
    vmem = pl.BlockSpec(memory_space=pltpu.VMEM)
    return pl.pallas_call(
        kernel,
        out_shape=outs,
        in_specs=[pl.BlockSpec(memory_space={"v": pltpu.VMEM, "s": pltpu.SMEM, "a": pl.ANY}[m]) for m in ins],
        out_specs=vmem if single else [vmem] * len(outs),
        scratch_shapes=list(scratch),
        compiler_params=pltpu.CompilerParams(vmem_limit_bytes=int(mib * 1024 * 1024)),
    )


def main(*args):
    s = jax.ShapeDtypeStruct
    v = pltpu.VMEM
    return call(
        body,
        "vvvvvvvv",
        [s((128, C), BF16), s((ACT, 3 * C), BF16), s((ACT, 3 * C), BF16)],
        [v((384, C), F32), v((384, 1), F32), v((320, C), F32), v((320, C), BF16), v((320, 2 * C), F32),
         v((320, C), F32), v((320, C), F32), v((320, 1), F32), v((256, C), F32), v((256, C), BF16),
         v((256, 2 * C), F32), v((256, 2 * C), BF16), v((256, C), F32), v((128, C), F32),
         v((192, 2 * C), BF16), v((192, C), F32), v((2, ACT, 3 * C), BF16)],
    )(*args)


def shards(tokens, cotangent, gaps, taps, gains, proj):
    tok, cot = tokens[0], cotangent[0]
    n = 128
    s = jax.ShapeDtypeStruct
    far = [pltpu.with_memory_space_constraint(a, pltpu.HBM) for a in (gaps, tok, cot)]
    up, down = call(pack, "svv", [s((192, C), BF16), s((192, C), BF16)], mib=48)(*far)
    prev = lax.ppermute(up, SEQ, [(i, i + 1) for i in range(n - 1)])
    nxt = lax.ppermute(down, SEQ, [(i + 1, i) for i in range(n - 1)])
    here = [jnp.transpose(taps, (1, 0, 2)), gains, proj]
    here = far + [pltpu.with_memory_space_constraint(a, pltpu.HBM) for a in here]
    near_args = call(
        warm,
        "svvvvv",
        [s((128, 1), F32), s((128, C), BF16), s((128, C), BF16), s((3, 2, C), F32), s((2, C), F32),
         s((2, C, 2 * C), BF16)],
    )(*here)
    tokens_grad, keep, send = main(near_args[0], prev, nxt, *near_args[1:])
    recv = lax.ppermute(send, "c", [(0, 1), (1, 0)])
    pick, mine = call(own_terms, "v", [s((C, C), BF16), s((C, 2 * C), F32)])(keep)
    part = call(terms, "vvvv", s((8, 528, 128), BF16))(keep, recv, pick, mine)
    part = lax.all_to_all(part, ALL, 0, 0, axis_index_groups=NEAR, tiled=True)
    part = call(first_sum, "v", s((32, 32, 128), BF16))(part)
    part = lax.all_to_all(part, ALL, 0, 0, axis_index_groups=FAR, tiled=True)
    part = call(second_sum, "v", s((32, 128), F32))(part)
    part = lax.all_gather(part, HAP, axis=0)
    projection_grad, taps_grad, gains_grad = call(
        place, "v", [s((2, 4, 1024), F32), s((3, 2, C), F32), s((2, C), F32)]
    )(part)
    return tokens_grad[None], projection_grad, jnp.transpose(taps_grad, (1, 0, 2)), gains_grad


def solution(mesh):
    fine = Mesh(mesh.devices.reshape(8, 4, 4, 2, 2), ("z", "x", "yh", "yl", "c"))
    return jax.shard_map(
        shards,
        mesh=fine,
        in_specs=(P(HAP, SEQ, None), P(HAP, SEQ, None), P(SEQ, None), P(), P(), P()),
        out_specs=(P(HAP, SEQ, None), P(None, SEQ, None), P(), P()),
        check_vma=False,
    )
```

```python
import jax
import jax.numpy as jnp
from jax import lax
from jax.experimental import pallas as pl
from jax.experimental.pallas import tpu as pltpu
from jax.sharding import Mesh
from jax.sharding import PartitionSpec as P

C = 512
DIL = 32
EPS = 1e-06
F32 = jnp.float32
BF16 = jnp.bfloat16
ALL = ("z", "x", "yh", "yl", "c")
SEQ = ("z", "x", "yh")
HAP = ("yl", "c")
G0 = 0.7978845608028654
G1 = 0.044715
MARK = 64.0
ACT = 144


def gelu_and_slope(x, with_slope=True):
    x2 = x * x
    cdf = 0.5 + 0.5 * jnp.tanh(x * (G0 + (G0 * G1) * x2))
    hid = x * cdf
    if not with_slope:
        return hid, None
    return hid, cdf + hid * (1.0 - cdf) * (2.0 * G0 + (6.0 * G0 * G1) * x2)


def sigmoid(x):
    return 0.5 + 0.5 * jnp.tanh(0.5 * x)


def dot(a, b, dims):
    return lax.dot_general(a, b, (dims, ((), ())), preferred_element_type=F32)


def fold8(v):
    return jnp.sum(v.reshape(v.shape[0] // 8, 8, v.shape[1]), axis=0)


def hi_lo(v):
    hi = v.astype(BF16)
    lo = (v - hi.astype(F32)).astype(BF16)
    return hi, lo


def pack(gaps, tok, cot, up, down):
    at = lax.broadcasted_iota(jnp.int32, (128, 1), 0)
    inside = (at >= gaps[0, 0]) & (at < gaps[0, 1])
    marked = jnp.where(inside, MARK, tok[...].astype(F32)).astype(BF16)
    up[0:128, :] = marked
    down[0:128, :] = marked
    up[128:192, :] = cot[64:128, :]
    down[128:192, :] = cot[0:64, :]


def warm(gaps, tok, cot, taps, gains, proj, valid, tok_out, cot_out, taps_out, gains_out, proj_out):
    at = lax.broadcasted_iota(jnp.int32, (128, 1), 0)
    valid[...] = jnp.where((at >= gaps[0, 0]) & (at < gaps[0, 1]), 0.0, 1.0)
    for a, b in ((tok, tok_out), (cot, cot_out), (taps, taps_out), (gains, gains_out), (proj, proj_out)):
        b[...] = a[...]


def body(own_valid, prev, nxt, tok, cot, taps, gains, proj, out, keep, send,
         n0, i0, g0, h0, ab0, x1, n1, i1, g1, h1, po1, dp1, dh1, gr1, dp0, dh0, act):
    core = lax.axis_index("c")
    place_in_seq = sum(lax.axis_index(a) for a in SEQ)
    inner = (place_in_seq > 0, None, place_in_seq < 13)

    def rows(base):
        ref, at = ((prev, base), (tok, base - 128), (nxt, base - 256))[base // 128]
        return ref[at:at + DIL, :].astype(F32)

    def cot_rows(base):
        if base < 128:
            return prev[128 + base - 64:128 + base - 32, :].astype(F32)
        if base < 256:
            return cot[base - 128:base - 96, :].astype(F32)
        return nxt[128 + base - 256:128 + base - 224, :].astype(F32)

    valid_of = []
    for chunk in range(12):
        if 4 <= chunk < 8:
            valid_of.append(own_valid[DIL * (chunk - 4):DIL * (chunk - 3), :])
        else:
            ref = prev if chunk < 4 else nxt
            lead = ref[DIL * (chunk % 4):DIL * (chunk % 4) + DIL, 0:128].astype(F32)[:, 0:1]
            valid_of.append(jnp.where(lead < 0.5 * MARK, jnp.where(inner[chunk // 4], 1.0, 0.0), 0.0))

    def norm(v, valid, gain):
        inv = lax.rsqrt(jnp.sum(v * v, axis=-1, keepdims=True) * (1.0 / C) + EPS)
        return inv, v * (inv * valid) * gain

    def tap(layer, k):
        return taps[k, layer:layer + 1, :]

    def conv(ref, at, layer):
        return (tap(layer, 0) * ref[at - DIL:at, :] + tap(layer, 1) * ref[at:at + DIL, :]
                + tap(layer, 2) * ref[at + DIL:at + 2 * DIL, :])

    for c in range(12):
        inv, normed = norm(rows(c * DIL), valid_of[c], gains[0:1, :])
        if 4 <= c < 8:
            i0[c * DIL:(c + 1) * DIL, :] = inv
        n0[c * DIL:(c + 1) * DIL, :] = normed
    for c in range(1, 11):
        hid, slope = gelu_and_slope(conv(n0, c * DIL, 0), 3 <= c < 9)
        h0[(c - 1) * DIL:c * DIL, :] = hid.astype(BF16)
        if 3 <= c < 9:
            g0[(c - 1) * DIL:c * DIL, :] = slope
    ab0[...] = dot(h0[...], proj[0], ((1,), (0,)))
    for c in range(1, 11):
        at = slice((c - 1) * DIL, c * DIL)
        first = ab0[at, 0:C]
        gate = sigmoid(ab0[at, C:2 * C])
        both = first * gate
        nx = (rows(c * DIL) + valid_of[c] * both).astype(BF16).astype(F32)
        inv, normed = norm(nx, valid_of[c], gains[1:2, :])
        if 3 <= c < 9:
            ab0[at, 0:C] = gate
            ab0[at, C:2 * C] = both * (1.0 - gate)
            x1[at, :] = nx
            i1[at, :] = inv
        n1[at, :] = normed
    for c in range(2, 10):
        hid, slope = gelu_and_slope(conv(n1, (c - 1) * DIL, 1))
        h1[(c - 2) * DIL:(c - 1) * DIL, :] = hid.astype(BF16)
        g1[(c - 2) * DIL:(c - 1) * DIL, :] = slope
    po1[...] = dot(h1[...], proj[1], ((1,), (0,)))
    for c in range(2, 10):
        at = slice((c - 2) * DIL, (c - 1) * DIL)
        first = po1[at, 0:C]
        gate = sigmoid(po1[at, C:2 * C])
        bg = valid_of[c] * cot_rows(c * DIL) * gate
        dp1[at, 0:C] = bg.astype(BF16)
        dp1[at, C:2 * C] = (bg * first * (1.0 - gate)).astype(BF16)
    dh1[...] = dot(dp1[...], proj[1], ((1,), (1,))) * g1[...]

    def back(dref, c_off, layer, c, sref_rows, inv, valid, gain):
        at = c_off
        dn = (tap(layer, 0) * dref[at + DIL:at + 2 * DIL, :] + tap(layer, 1) * dref[at:at + DIL, :]
              + tap(layer, 2) * dref[at - DIL:at, :])
        dq = dn * valid
        si = sref_rows * inv
        qs = dq * si
        dt = dq * gain
        m = jnp.sum(qs * gain, axis=-1, keepdims=True) * (1.0 / C)
        return inv * (dt - si * m), qs

    def small_rows(parts):
        return [jnp.sum(p, axis=0, keepdims=True) for p in parts]

    acc = [jnp.zeros((8, C), F32) for _ in range(4)]
    for c in range(3, 9):
        at1 = slice((c - 1) * DIL, c * DIL)
        delta, qs = back(dh1, (c - 2) * DIL, 1, c, x1[at1, :], i1[at1, :], valid_of[c], gains[1:2, :])
        grad = cot_rows(c * DIL) + delta
        branch = valid_of[c] * grad
        to = slice((c - 3) * DIL, (c - 2) * DIL)
        dp0[to, 0:C] = (branch * ab0[at1, 0:C]).astype(BF16)
        dp0[to, C:2 * C] = (branch * ab0[at1, C:2 * C]).astype(BF16)
        if 4 <= c < 8:
            gr1[(c - 4) * DIL:(c - 3) * DIL, :] = grad
            d = dh1[(c - 2) * DIL:(c - 1) * DIL, :]
            for k in range(3):
                acc[k] += fold8(d * n1[(c - 2 + k) * DIL:(c - 1 + k) * DIL, :])
            acc[3] += fold8(qs)

    def put(layer, hid, dpr, parts):
        act[layer, 0:128, 0:C] = hid
        act[layer, 0:128, C:3 * C] = dpr
        four = jnp.concatenate(small_rows(parts) + [jnp.zeros((12, C), F32)], axis=0)
        hi, lo = hi_lo(four)
        act[layer, 128:ACT, 0:C] = hi
        act[layer, 128:ACT, C:2 * C] = lo
        act[layer, 128:ACT, 2 * C:3 * C] = jnp.zeros((16, C), BF16)

    put(1, h1[64:192, :], dp1[64:192, :], acc)

    dh0[...] = dot(dp0[...], proj[0], ((1,), (1,))) * g0[64:256, :]
    acc = [jnp.zeros((8, C), F32) for _ in range(4)]
    for c in range(4, 8):
        delta, qs = back(dh0, (c - 3) * DIL, 0, c, rows(c * DIL), i0[c * DIL:(c + 1) * DIL, :],
                         valid_of[c], gains[0:1, :])
        at = slice((c - 4) * DIL, (c - 3) * DIL)
        out[at, :] = (gr1[at, :] + delta).astype(BF16)
        d = dh0[(c - 3) * DIL:(c - 2) * DIL, :]
        for k in range(3):
            acc[k] += fold8(d * n0[(c - 1 + k) * DIL:(c + k) * DIL, :])
        acc[3] += fold8(qs)
    put(0, h0[96:224, :], dp0[32:160, :], acc)
    keep[...] = act[core]
    send[...] = act[1 - core]


def device(near, far, core):
    z = ((far >> 3) * 2 + (near >> 2) + core) % 8
    x = ((far >> 2) % 2 * 2 + (near >> 1) % 2 + core) % 4
    y = (far % 4 * 2 + near % 2 + core) % 8
    return ((z * 4 + x) * 8 + y) * 2 + core


NEAR = [[device(n, f, c) for n in range(8)] for c in range(2) for f in range(32)]
FAR = [[device(n, f, c) for f in range(32)] for c in range(2) for n in range(8)]


def own_terms(keep, pick, mine):
    core = lax.axis_index("c")
    q = lax.broadcasted_iota(jnp.int32, (C, 1), 0)
    z = ((((q >> 5) & 1) << 2 | ((q >> 4) & 1) << 1 | ((q >> 8) & 1)) + core) & 7
    x = ((((q >> 3) & 1) << 1 | ((q >> 7) & 1)) + core) & 3
    y = ((((q >> 1) & 3) << 1 | ((q >> 6) & 1)) + core) & 7
    ch = z << 6 | x << 4 | y << 1 | (q & 1)
    pick[...] = (ch == lax.broadcasted_iota(jnp.int32, (C, C), 1)).astype(F32).astype(BF16)
    ha = dot(pick[...], keep[0:128, 0:C], ((1,), (1,))).astype(BF16)
    mine[...] = dot(ha, keep[0:128, C:3 * C], ((1,), (0,)))


def terms(keep, recv, pick, mine, out):
    hb = dot(pick[...], recv[0:128, 0:C], ((1,), (1,))).astype(BF16)
    for j in range(8):
        cols = slice(j * 128, (j + 1) * 128)
        t = mine[:, cols] + dot(hb, recv[0:128, C + j * 128:C + (j + 1) * 128], ((1,), (0,)))
        out[:, j * 64:(j + 1) * 64, :] = t.astype(BF16).reshape(8, 64, 128)
    small = (keep[128:ACT, 0:C].astype(F32) + keep[128:ACT, C:2 * C].astype(F32)
             + recv[128:ACT, 0:C].astype(F32) + recv[128:ACT, C:2 * C].astype(F32))
    tile = jnp.concatenate(
        [small[r:r + 1, 128 * q:128 * (q + 1)] for r in range(4) for q in range(4)], axis=0).astype(BF16)
    for g in range(8):
        out[g, 512:528, :] = tile


def first_sum(recv, out):
    total = recv[0].astype(F32)
    for i in range(1, 8):
        total += recv[i].astype(F32)
    p = lax.broadcasted_iota(jnp.int32, (C, 1), 0)
    src = ((p >> 1) & 7) << 6 | (p >> 4) << 1 | (p & 1)
    pick = (src == lax.broadcasted_iota(jnp.int32, (C, C), 1)).astype(F32).astype(BF16)
    moved = dot(pick, total[0:512, :].astype(BF16), ((1,), (0,)))
    half = jnp.where(lax.axis_index("yl") == 0, total[512:520, :], total[520:528, :])
    for d in range(32):
        out[d] = jnp.concatenate([moved[16 * d:16 * d + 16, :], half], axis=0).astype(BF16)


def second_sum(recv, out):
    total = recv[0].astype(F32)
    for i in range(1, 32):
        total += recv[i].astype(F32)
    out[...] = total


def place(recv, proj, taps, gains):
    for c in range(2):
        for y in range(2):
            for j in range(8):
                proj[c, 2 * y:2 * y + 2, j * 128:(j + 1) * 128] = recv[y * 2 + c, 2 * j:2 * j + 2, :]
        for r in range(4):
            for q in range(4):
                at = 16 + (r % 2) * 4 + q
                row = recv[(r // 2) * 2 + c, at:at + 1, :]
                if r < 3:
                    taps[r, c:c + 1, q * 128:(q + 1) * 128] = row
                else:
                    gains[c:c + 1, q * 128:(q + 1) * 128] = row


def call(kernel, ins, outs, scratch=(), mib=48):
    single = not isinstance(outs, (list, tuple))
    vmem = pl.BlockSpec(memory_space=pltpu.VMEM)
    return pl.pallas_call(
        kernel,
        out_shape=outs,
        in_specs=[pl.BlockSpec(memory_space={"v": pltpu.VMEM, "s": pltpu.SMEM, "a": pl.ANY}[m]) for m in ins],
        out_specs=vmem if single else [vmem] * len(outs),
        scratch_shapes=list(scratch),
        compiler_params=pltpu.CompilerParams(vmem_limit_bytes=int(mib * 1024 * 1024)),
    )


def main(*args):
    s = jax.ShapeDtypeStruct
    v = pltpu.VMEM
    return call(
        body,
        "vvvvvvvv",
        [s((128, C), BF16), s((ACT, 3 * C), BF16), s((ACT, 3 * C), BF16)],
        [v((384, C), F32), v((384, 1), F32), v((320, C), F32), v((320, C), BF16), v((320, 2 * C), F32),
         v((320, C), F32), v((320, C), F32), v((320, 1), F32), v((256, C), F32), v((256, C), BF16),
         v((256, 2 * C), F32), v((256, 2 * C), BF16), v((256, C), F32), v((128, C), F32),
         v((192, 2 * C), BF16), v((192, C), F32), v((2, ACT, 3 * C), BF16)],
    )(*args)


def shards(tokens, cotangent, gaps, taps, gains, proj):
    tok, cot = tokens[0], cotangent[0]
    n = 128
    s = jax.ShapeDtypeStruct
    far = [pltpu.with_memory_space_constraint(a, pltpu.HBM) for a in (gaps, tok, cot)]
    up, down = call(pack, "svv", [s((192, C), BF16), s((192, C), BF16)], mib=48)(*far)
    prev = lax.ppermute(up, SEQ, [(i, i + 1) for i in range(n - 1)])
    nxt = lax.ppermute(down, SEQ, [(i + 1, i) for i in range(n - 1)])
    here = [jnp.transpose(taps, (1, 0, 2)), gains, proj]
    here = far + [pltpu.with_memory_space_constraint(a, pltpu.HBM) for a in here]
    near_args = call(
        warm,
        "svvvvv",
        [s((128, 1), F32), s((128, C), BF16), s((128, C), BF16), s((3, 2, C), F32), s((2, C), F32),
         s((2, C, 2 * C), BF16)],
    )(*here)
    tokens_grad, keep, send = main(near_args[0], prev, nxt, *near_args[1:])
    recv = lax.ppermute(send, "c", [(0, 1), (1, 0)])
    pick, mine = call(own_terms, "v", [s((C, C), BF16), s((C, 2 * C), F32)])(keep)
    part = call(terms, "vvvv", s((8, 528, 128), BF16))(keep, recv, pick, mine)
    part = lax.all_to_all(part, ALL, 0, 0, axis_index_groups=NEAR, tiled=True)
    part = call(first_sum, "v", s((32, 24, 128), BF16))(part)
    part = lax.all_to_all(part, ALL, 0, 0, axis_index_groups=FAR, tiled=True)
    part = call(second_sum, "v", s((24, 128), F32))(part)
    part = lax.all_gather(part, HAP, axis=0)
    projection_grad, taps_grad, gains_grad = call(
        place, "v", [s((2, 4, 1024), F32), s((3, 2, C), F32), s((2, C), F32)]
    )(part)
    return tokens_grad[None], projection_grad, jnp.transpose(taps_grad, (1, 0, 2)), gains_grad


def solution(mesh):
    fine = Mesh(mesh.devices.reshape(8, 4, 4, 2, 2), ("z", "x", "yh", "yl", "c"))
    return jax.shard_map(
        shards,
        mesh=fine,
        in_specs=(P(HAP, SEQ, None), P(HAP, SEQ, None), P(SEQ, None), P(), P(), P()),
        out_specs=(P(HAP, SEQ, None), P(None, SEQ, None), P(), P()),
        check_vma=False,
    )
```

```python
import jax
import jax.numpy as jnp
from jax import lax
from jax.experimental import pallas as pl
from jax.experimental.pallas import tpu as pltpu
from jax.sharding import Mesh
from jax.sharding import PartitionSpec as P

C = 512
DIL = 32
EPS = 1e-06
F32 = jnp.float32
BF16 = jnp.bfloat16
ALL = ("z", "xh", "xl", "yh", "yl", "c")
LAST = ("xh", "yl", "c")
SEQ = ("z", "xh", "xl", "yh")
HAP = ("yl", "c")
G0 = 0.7978845608028654
G1 = 0.044715
MARK = 64.0
ACT = 144


def gelu_and_slope(x, with_slope=True):
    x2 = x * x
    cdf = 0.5 + 0.5 * jnp.tanh(x * (G0 + (G0 * G1) * x2))
    hid = x * cdf
    if not with_slope:
        return hid, None
    return hid, cdf + hid * (1.0 - cdf) * (2.0 * G0 + (6.0 * G0 * G1) * x2)


def sigmoid(x):
    return 0.5 + 0.5 * jnp.tanh(0.5 * x)


def dot(a, b, dims):
    return lax.dot_general(a, b, (dims, ((), ())), preferred_element_type=F32)


def fold8(v):
    return jnp.sum(v.reshape(v.shape[0] // 8, 8, v.shape[1]), axis=0)


def hi_lo(v):
    hi = v.astype(BF16)
    lo = (v - hi.astype(F32)).astype(BF16)
    return hi, lo


def pack(gaps, tok, cot, up, down):
    at = lax.broadcasted_iota(jnp.int32, (128, 1), 0)
    inside = (at >= gaps[0, 0]) & (at < gaps[0, 1])
    marked = jnp.where(inside, MARK, tok[...].astype(F32)).astype(BF16)
    up[0:128, :] = marked
    down[0:128, :] = marked
    up[128:192, :] = cot[64:128, :]
    down[128:192, :] = cot[0:64, :]


def warm(gaps, tok, cot, taps, gains, proj, valid, tok_out, cot_out, taps_out, gains_out, proj_out):
    at = lax.broadcasted_iota(jnp.int32, (128, 1), 0)
    valid[...] = jnp.where((at >= gaps[0, 0]) & (at < gaps[0, 1]), 0.0, 1.0)
    for a, b in ((tok, tok_out), (cot, cot_out), (taps, taps_out), (gains, gains_out), (proj, proj_out)):
        b[...] = a[...]


def body(own_valid, prev, nxt, tok, cot, taps, gains, proj, out, keep, send,
         n0, i0, g0, h0, ab0, x1, n1, i1, g1, h1, po1, dp1, dh1, gr1, dp0, dh0, act):
    core = lax.axis_index("c")
    place_in_seq = sum(lax.axis_index(a) for a in SEQ)
    inner = (place_in_seq > 0, None, place_in_seq < 12)

    def rows(base):
        ref, at = ((prev, base), (tok, base - 128), (nxt, base - 256))[base // 128]
        return ref[at:at + DIL, :].astype(F32)

    def cot_rows(base):
        if base < 128:
            return prev[128 + base - 64:128 + base - 32, :].astype(F32)
        if base < 256:
            return cot[base - 128:base - 96, :].astype(F32)
        return nxt[128 + base - 256:128 + base - 224, :].astype(F32)

    valid_of = []
    for chunk in range(12):
        if 4 <= chunk < 8:
            valid_of.append(own_valid[DIL * (chunk - 4):DIL * (chunk - 3), :])
        else:
            ref = prev if chunk < 4 else nxt
            lead = ref[DIL * (chunk % 4):DIL * (chunk % 4) + DIL, 0:128].astype(F32)[:, 0:1]
            valid_of.append(jnp.where(lead < 0.5 * MARK, jnp.where(inner[chunk // 4], 1.0, 0.0), 0.0))

    def norm(v, valid, gain):
        inv = lax.rsqrt(jnp.sum(v * v, axis=-1, keepdims=True) * (1.0 / C) + EPS)
        return inv, v * (inv * valid) * gain

    def tap(layer, k):
        return taps[k, layer:layer + 1, :]

    def conv(ref, at, layer):
        return (tap(layer, 0) * ref[at - DIL:at, :] + tap(layer, 1) * ref[at:at + DIL, :]
                + tap(layer, 2) * ref[at + DIL:at + 2 * DIL, :])

    for c in range(12):
        inv, normed = norm(rows(c * DIL), valid_of[c], gains[0:1, :])
        if 4 <= c < 8:
            i0[c * DIL:(c + 1) * DIL, :] = inv
        n0[c * DIL:(c + 1) * DIL, :] = normed
    for c in range(1, 11):
        hid, slope = gelu_and_slope(conv(n0, c * DIL, 0), 3 <= c < 9)
        h0[(c - 1) * DIL:c * DIL, :] = hid.astype(BF16)
        if 3 <= c < 9:
            g0[(c - 1) * DIL:c * DIL, :] = slope
    ab0[...] = dot(h0[...], proj[0], ((1,), (0,)))
    for c in range(1, 11):
        at = slice((c - 1) * DIL, c * DIL)
        first = ab0[at, 0:C]
        gate = sigmoid(ab0[at, C:2 * C])
        both = first * gate
        nx = (rows(c * DIL) + valid_of[c] * both).astype(BF16).astype(F32)
        inv, normed = norm(nx, valid_of[c], gains[1:2, :])
        if 3 <= c < 9:
            ab0[at, 0:C] = gate
            ab0[at, C:2 * C] = both * (1.0 - gate)
            x1[at, :] = nx
            i1[at, :] = inv
        n1[at, :] = normed
    for c in range(2, 10):
        hid, slope = gelu_and_slope(conv(n1, (c - 1) * DIL, 1))
        h1[(c - 2) * DIL:(c - 1) * DIL, :] = hid.astype(BF16)
        g1[(c - 2) * DIL:(c - 1) * DIL, :] = slope
    po1[...] = dot(h1[...], proj[1], ((1,), (0,)))
    for c in range(2, 10):
        at = slice((c - 2) * DIL, (c - 1) * DIL)
        first = po1[at, 0:C]
        gate = sigmoid(po1[at, C:2 * C])
        bg = valid_of[c] * cot_rows(c * DIL) * gate
        dp1[at, 0:C] = bg.astype(BF16)
        dp1[at, C:2 * C] = (bg * first * (1.0 - gate)).astype(BF16)
    dh1[...] = dot(dp1[...], proj[1], ((1,), (1,))) * g1[...]

    def back(dref, c_off, layer, c, sref_rows, inv, valid, gain):
        at = c_off
        dn = (tap(layer, 0) * dref[at + DIL:at + 2 * DIL, :] + tap(layer, 1) * dref[at:at + DIL, :]
              + tap(layer, 2) * dref[at - DIL:at, :])
        dq = dn * valid
        si = sref_rows * inv
        qs = dq * si
        dt = dq * gain
        m = jnp.sum(qs * gain, axis=-1, keepdims=True) * (1.0 / C)
        return inv * (dt - si * m), qs

    def small_rows(parts):
        return [jnp.sum(p, axis=0, keepdims=True) for p in parts]

    acc = [jnp.zeros((8, C), F32) for _ in range(4)]
    for c in range(3, 9):
        at1 = slice((c - 1) * DIL, c * DIL)
        delta, qs = back(dh1, (c - 2) * DIL, 1, c, x1[at1, :], i1[at1, :], valid_of[c], gains[1:2, :])
        grad = cot_rows(c * DIL) + delta
        branch = valid_of[c] * grad
        to = slice((c - 3) * DIL, (c - 2) * DIL)
        dp0[to, 0:C] = (branch * ab0[at1, 0:C]).astype(BF16)
        dp0[to, C:2 * C] = (branch * ab0[at1, C:2 * C]).astype(BF16)
        if 4 <= c < 8:
            gr1[(c - 4) * DIL:(c - 3) * DIL, :] = grad
            d = dh1[(c - 2) * DIL:(c - 1) * DIL, :]
            for k in range(3):
                acc[k] += fold8(d * n1[(c - 2 + k) * DIL:(c - 1 + k) * DIL, :])
            acc[3] += fold8(qs)

    def put(layer, hid, dpr, parts):
        act[layer, 0:128, 0:C] = hid
        act[layer, 0:128, C:3 * C] = dpr
        four = jnp.concatenate(small_rows(parts) + [jnp.zeros((12, C), F32)], axis=0)
        hi, lo = hi_lo(four)
        act[layer, 128:ACT, 0:C] = hi
        act[layer, 128:ACT, C:2 * C] = lo
        act[layer, 128:ACT, 2 * C:3 * C] = jnp.zeros((16, C), BF16)

    put(1, h1[64:192, :], dp1[64:192, :], acc)

    dh0[...] = dot(dp0[...], proj[0], ((1,), (1,))) * g0[64:256, :]
    acc = [jnp.zeros((8, C), F32) for _ in range(4)]
    for c in range(4, 8):
        delta, qs = back(dh0, (c - 3) * DIL, 0, c, rows(c * DIL), i0[c * DIL:(c + 1) * DIL, :],
                         valid_of[c], gains[0:1, :])
        at = slice((c - 4) * DIL, (c - 3) * DIL)
        out[at, :] = (gr1[at, :] + delta).astype(BF16)
        d = dh0[(c - 3) * DIL:(c - 2) * DIL, :]
        for k in range(3):
            acc[k] += fold8(d * n0[(c - 1 + k) * DIL:(c + k) * DIL, :])
        acc[3] += fold8(qs)
    put(0, h0[96:224, :], dp0[32:160, :], acc)
    keep[...] = act[core]
    send[...] = act[1 - core]


def device(near, far, core):
    z = ((far >> 3) * 2 + (near >> 2) + core) % 8
    x = ((far >> 2) % 2 * 2 + (near >> 1) % 2 + core) % 4
    y = (far % 4 * 2 + near % 2 + core) % 8
    return ((z * 4 + x) * 8 + y) * 2 + core


NEAR = [[device(n, f, c) for n in range(8)] for c in range(2) for f in range(32)]
FAR = [[device(n, (g >> 2) << 3 | x << 2 | g % 4, c) for g in range(16)] for c in range(2) for n in range(8) for x in range(2)]


def own_terms(keep, pick, mine):
    core = lax.axis_index("c")
    q = lax.broadcasted_iota(jnp.int32, (C, 1), 0)
    z = ((((q >> 5) & 1) << 2 | ((q >> 4) & 1) << 1 | ((q >> 8) & 1)) + core) & 7
    x = ((((q >> 3) & 1) << 1 | ((q >> 7) & 1)) + core) & 3
    y = ((((q >> 1) & 3) << 1 | ((q >> 6) & 1)) + core) & 7
    ch = z << 6 | x << 4 | y << 1 | (q & 1)
    pick[...] = (ch == lax.broadcasted_iota(jnp.int32, (C, C), 1)).astype(F32).astype(BF16)
    ha = dot(pick[...], keep[0:128, 0:C], ((1,), (1,))).astype(BF16)
    mine[...] = dot(ha, keep[0:128, C:3 * C], ((1,), (0,)))


def terms(keep, recv, pick, mine, out):
    hb = dot(pick[...], recv[0:128, 0:C], ((1,), (1,))).astype(BF16)
    for j in range(8):
        cols = slice(j * 128, (j + 1) * 128)
        t = mine[:, cols] + dot(hb, recv[0:128, C + j * 128:C + (j + 1) * 128], ((1,), (0,)))
        out[:, j * 64:(j + 1) * 64, :] = t.astype(BF16).reshape(8, 64, 128)
    small = (keep[128:ACT, 0:C].astype(F32) + keep[128:ACT, C:2 * C].astype(F32)
             + recv[128:ACT, 0:C].astype(F32) + recv[128:ACT, C:2 * C].astype(F32))
    tile = jnp.concatenate(
        [small[r:r + 1, 128 * q:128 * (q + 1)] for r in range(4) for q in range(4)], axis=0).astype(BF16)
    for g in range(8):
        out[g, 512:528, :] = tile


def first_sum(recv, out):
    total = recv[0].astype(F32)
    for i in range(1, 8):
        total += recv[i].astype(F32)
    p = lax.broadcasted_iota(jnp.int32, (C, 1), 0)
    src = ((p >> 1) & 7) << 6 | ((p >> 7) & 3) << 4 | ((p >> 4) & 1) << 3 | ((p >> 5) & 3) << 1 | (p & 1)
    pick = (src == lax.broadcasted_iota(jnp.int32, (C, C), 1)).astype(F32).astype(BF16)
    moved = dot(pick, total[0:512, :].astype(BF16), ((1,), (0,)))
    half = jnp.where(lax.axis_index("yl") == 0, total[512:520, :], total[520:528, :])
    for d in range(16):
        out[d] = jnp.concatenate([moved[32 * d:32 * d + 32, :], half], axis=0).astype(BF16)


def second_sum(recv, out):
    total = recv[0].astype(F32)
    for i in range(1, 16):
        total += recv[i].astype(F32)
    swap = (lax.axis_index("c") == 1) & (lax.axis_index("xl") == 0)
    a, b = total[0:16, :], total[16:32, :]
    for i in range(8):
        piece = jnp.where(swap, b, a) if i < 4 else jnp.where(swap, a, b)
        out[i] = jnp.concatenate([piece, total[32:40, :]], axis=0)


def place(recv, proj, taps, gains):
    for c in range(2):
        for y in range(2):
            for j in range(8):
                proj[c, 2 * y:2 * y + 2, j * 128:(j + 1) * 128] = recv[y * 2 + c, 2 * j:2 * j + 2, :] + recv[4 + y * 2 + c, 2 * j:2 * j + 2, :]
        for r in range(4):
            for q in range(4):
                at = 16 + (r % 2) * 4 + q
                row = recv[(r // 2) * 2 + c, at:at + 1, :] + recv[4 + (r // 2) * 2 + c, at:at + 1, :]
                if r < 3:
                    taps[r, c:c + 1, q * 128:(q + 1) * 128] = row
                else:
                    gains[c:c + 1, q * 128:(q + 1) * 128] = row


def call(kernel, ins, outs, scratch=(), mib=48):
    single = not isinstance(outs, (list, tuple))
    vmem = pl.BlockSpec(memory_space=pltpu.VMEM)
    return pl.pallas_call(
        kernel,
        out_shape=outs,
        in_specs=[pl.BlockSpec(memory_space={"v": pltpu.VMEM, "s": pltpu.SMEM, "a": pl.ANY}[m]) for m in ins],
        out_specs=vmem if single else [vmem] * len(outs),
        scratch_shapes=list(scratch),
        compiler_params=pltpu.CompilerParams(vmem_limit_bytes=int(mib * 1024 * 1024)),
    )


def main(*args):
    s = jax.ShapeDtypeStruct
    v = pltpu.VMEM
    return call(
        body,
        "vvvvvvvv",
        [s((128, C), BF16), s((ACT, 3 * C), BF16), s((ACT, 3 * C), BF16)],
        [v((384, C), F32), v((384, 1), F32), v((320, C), F32), v((320, C), BF16), v((320, 2 * C), F32),
         v((320, C), F32), v((320, C), F32), v((320, 1), F32), v((256, C), F32), v((256, C), BF16),
         v((256, 2 * C), F32), v((256, 2 * C), BF16), v((256, C), F32), v((128, C), F32),
         v((192, 2 * C), BF16), v((192, C), F32), v((2, ACT, 3 * C), BF16)],
    )(*args)


def shards(tokens, cotangent, gaps, taps, gains, proj):
    tok, cot = tokens[0], cotangent[0]
    n = 128
    s = jax.ShapeDtypeStruct
    far = [pltpu.with_memory_space_constraint(a, pltpu.HBM) for a in (gaps, tok, cot)]
    up, down = call(pack, "svv", [s((192, C), BF16), s((192, C), BF16)], mib=48)(*far)
    prev = lax.ppermute(up, SEQ, [(i, i + 1) for i in range(n - 1)])
    nxt = lax.ppermute(down, SEQ, [(i + 1, i) for i in range(n - 1)])
    here = [jnp.transpose(taps, (1, 0, 2)), gains, proj]
    here = far + [pltpu.with_memory_space_constraint(a, pltpu.HBM) for a in here]
    near_args = call(
        warm,
        "svvvvv",
        [s((128, 1), F32), s((128, C), BF16), s((128, C), BF16), s((3, 2, C), F32), s((2, C), F32),
         s((2, C, 2 * C), BF16)],
    )(*here)
    tokens_grad, keep, send = main(near_args[0], prev, nxt, *near_args[1:])
    recv = lax.ppermute(send, "c", [(0, 1), (1, 0)])
    pick, mine = call(own_terms, "v", [s((C, C), BF16), s((C, 2 * C), F32)])(keep)
    part = call(terms, "vvvv", s((8, 528, 128), BF16))(keep, recv, pick, mine)
    part = lax.all_to_all(part, ALL, 0, 0, axis_index_groups=NEAR, tiled=True)
    part = call(first_sum, "v", s((16, 40, 128), BF16))(part)
    part = lax.all_to_all(part, ALL, 0, 0, axis_index_groups=FAR, tiled=True)
    part = call(second_sum, "v", s((8, 24, 128), F32))(part)
    part = lax.all_to_all(part, LAST, 0, 0, tiled=True)
    projection_grad, taps_grad, gains_grad = call(
        place, "v", [s((2, 4, 1024), F32), s((3, 2, C), F32), s((2, C), F32)]
    )(part)
    return tokens_grad[None], projection_grad, jnp.transpose(taps_grad, (1, 0, 2)), gains_grad


def solution(mesh):
    fine = Mesh(mesh.devices.reshape(8, 2, 2, 4, 2, 2), ALL)
    return jax.shard_map(
        shards,
        mesh=fine,
        in_specs=(P(HAP, SEQ, None), P(HAP, SEQ, None), P(SEQ, None), P(), P(), P()),
        out_specs=(P(HAP, SEQ, None), P(None, SEQ, None), P(), P()),
        check_vma=False,
    )
```

```python
import jax
import jax.numpy as jnp
from jax import lax
from jax.experimental import pallas as pl
from jax.experimental.pallas import tpu as pltpu
from jax.sharding import Mesh
from jax.sharding import PartitionSpec as P

C = 512
DIL = 32
EPS = 1e-06
F32 = jnp.float32
BF16 = jnp.bfloat16
ALL = ("z", "xh", "xl", "yh", "yl", "c")
LAST = ("xh", "yl", "c")
SEQ = ("z", "xh", "xl", "yh")
HAP = ("yl", "c")
G0 = 0.7978845608028654
G1 = 0.044715
MARK = 64.0
ACT = 144


def gelu_and_slope(x, with_slope=True):
    x2 = x * x
    cdf = 0.5 + 0.5 * jnp.tanh(x * (G0 + (G0 * G1) * x2))
    hid = x * cdf
    if not with_slope:
        return hid, None
    return hid, cdf + hid * (1.0 - cdf) * (2.0 * G0 + (6.0 * G0 * G1) * x2)


def sigmoid(x):
    return 0.5 + 0.5 * jnp.tanh(0.5 * x)


def dot(a, b, dims):
    return lax.dot_general(a, b, (dims, ((), ())), preferred_element_type=F32)


def fold8(v):
    return jnp.sum(v.reshape(v.shape[0] // 8, 8, v.shape[1]), axis=0)


def hi_lo(v):
    hi = v.astype(BF16)
    lo = (v - hi.astype(F32)).astype(BF16)
    return hi, lo


def pack(gaps, tok, cot, down, up):
    at = lax.broadcasted_iota(jnp.int32, (128, 1), 0)
    inside = (at >= gaps[0, 0]) & (at < gaps[0, 1])
    marked = jnp.where(inside, MARK, tok[...].astype(F32)).astype(BF16)
    up[0:128, :] = marked
    down[0:128, :] = marked
    up[128:192, :] = cot[64:128, :]
    down[128:192, :] = cot[0:64, :]


def warm(gaps, tok, cot, taps, gains, proj, valid, tok_out, cot_out, taps_out, gains_out, proj_out):
    at = lax.broadcasted_iota(jnp.int32, (128, 1), 0)
    valid[...] = jnp.where((at >= gaps[0, 0]) & (at < gaps[0, 1]), 0.0, 1.0)
    for a, b in ((tok, tok_out), (cot, cot_out), (taps, taps_out), (gains, gains_out), (proj, proj_out)):
        b[...] = a[...]


def body(own_valid, nxt, prev, tok, cot, taps, gains, proj, out, keep, send,
         n0, i0, g0, h0, ab0, x1, n1, i1, g1, h1, po1, dp1, dh1, gr1, dp0, dh0, act):
    core = lax.axis_index("c")
    place_in_seq = sum(lax.axis_index(a) for a in SEQ)
    inner = (place_in_seq > 0, None, place_in_seq < 12)

    def rows(base):
        ref, at = ((prev, base), (tok, base - 128), (nxt, base - 256))[base // 128]
        return ref[at:at + DIL, :].astype(F32)

    def cot_rows(base):
        if base < 128:
            return prev[128 + base - 64:128 + base - 32, :].astype(F32)
        if base < 256:
            return cot[base - 128:base - 96, :].astype(F32)
        return nxt[128 + base - 256:128 + base - 224, :].astype(F32)

    valid_of = []
    for chunk in range(12):
        if 4 <= chunk < 8:
            valid_of.append(own_valid[DIL * (chunk - 4):DIL * (chunk - 3), :])
        else:
            ref = prev if chunk < 4 else nxt
            lead = ref[DIL * (chunk % 4):DIL * (chunk % 4) + DIL, 0:128].astype(F32)[:, 0:1]
            valid_of.append(jnp.where(lead < 0.5 * MARK, jnp.where(inner[chunk // 4], 1.0, 0.0), 0.0))

    def norm(v, valid, gain):
        inv = lax.rsqrt(jnp.sum(v * v, axis=-1, keepdims=True) * (1.0 / C) + EPS)
        return inv, v * (inv * valid) * gain

    def tap(layer, k):
        return taps[k, layer:layer + 1, :]

    def conv(ref, at, layer):
        return (tap(layer, 0) * ref[at - DIL:at, :] + tap(layer, 1) * ref[at:at + DIL, :]
                + tap(layer, 2) * ref[at + DIL:at + 2 * DIL, :])

    for c in range(12):
        inv, normed = norm(rows(c * DIL), valid_of[c], gains[0:1, :])
        if 4 <= c < 8:
            i0[c * DIL:(c + 1) * DIL, :] = inv
        n0[c * DIL:(c + 1) * DIL, :] = normed
    for c in range(1, 11):
        hid, slope = gelu_and_slope(conv(n0, c * DIL, 0), 3 <= c < 9)
        h0[(c - 1) * DIL:c * DIL, :] = hid.astype(BF16)
        if 3 <= c < 9:
            g0[(c - 1) * DIL:c * DIL, :] = slope
    ab0[...] = dot(h0[...], proj[0], ((1,), (0,)))
    for c in range(1, 11):
        at = slice((c - 1) * DIL, c * DIL)
        first = ab0[at, 0:C]
        gate = sigmoid(ab0[at, C:2 * C])
        both = first * gate
        nx = (rows(c * DIL) + valid_of[c] * both).astype(BF16).astype(F32)
        inv, normed = norm(nx, valid_of[c], gains[1:2, :])
        if 3 <= c < 9:
            ab0[at, 0:C] = gate
            ab0[at, C:2 * C] = both * (1.0 - gate)
            x1[at, :] = nx
            i1[at, :] = inv
        n1[at, :] = normed
    for c in range(2, 10):
        hid, slope = gelu_and_slope(conv(n1, (c - 1) * DIL, 1))
        h1[(c - 2) * DIL:(c - 1) * DIL, :] = hid.astype(BF16)
        g1[(c - 2) * DIL:(c - 1) * DIL, :] = slope
    po1[...] = dot(h1[...], proj[1], ((1,), (0,)))
    for c in range(2, 10):
        at = slice((c - 2) * DIL, (c - 1) * DIL)
        first = po1[at, 0:C]
        gate = sigmoid(po1[at, C:2 * C])
        bg = valid_of[c] * cot_rows(c * DIL) * gate
        dp1[at, 0:C] = bg.astype(BF16)
        dp1[at, C:2 * C] = (bg * first * (1.0 - gate)).astype(BF16)
    dh1[...] = dot(dp1[...], proj[1], ((1,), (1,))) * g1[...]

    def back(dref, c_off, layer, c, sref_rows, inv, valid, gain):
        at = c_off
        dn = (tap(layer, 0) * dref[at + DIL:at + 2 * DIL, :] + tap(layer, 1) * dref[at:at + DIL, :]
              + tap(layer, 2) * dref[at - DIL:at, :])
        dq = dn * valid
        si = sref_rows * inv
        qs = dq * si
        dt = dq * gain
        m = jnp.sum(qs * gain, axis=-1, keepdims=True) * (1.0 / C)
        return inv * (dt - si * m), qs

    def small_rows(parts):
        return [jnp.sum(p, axis=0, keepdims=True) for p in parts]

    acc = [jnp.zeros((8, C), F32) for _ in range(4)]
    for c in range(3, 9):
        at1 = slice((c - 1) * DIL, c * DIL)
        delta, qs = back(dh1, (c - 2) * DIL, 1, c, x1[at1, :], i1[at1, :], valid_of[c], gains[1:2, :])
        grad = cot_rows(c * DIL) + delta
        branch = valid_of[c] * grad
        to = slice((c - 3) * DIL, (c - 2) * DIL)
        dp0[to, 0:C] = (branch * ab0[at1, 0:C]).astype(BF16)
        dp0[to, C:2 * C] = (branch * ab0[at1, C:2 * C]).astype(BF16)
        if 4 <= c < 8:
            gr1[(c - 4) * DIL:(c - 3) * DIL, :] = grad
            d = dh1[(c - 2) * DIL:(c - 1) * DIL, :]
            for k in range(3):
                acc[k] += fold8(d * n1[(c - 2 + k) * DIL:(c - 1 + k) * DIL, :])
            acc[3] += fold8(qs)

    def put(layer, hid, dpr, parts):
        act[layer, 0:128, 0:C] = hid
        act[layer, 0:128, C:3 * C] = dpr
        four = jnp.concatenate(small_rows(parts) + [jnp.zeros((12, C), F32)], axis=0)
        hi, lo = hi_lo(four)
        act[layer, 128:ACT, 0:C] = hi
        act[layer, 128:ACT, C:2 * C] = lo
        act[layer, 128:ACT, 2 * C:3 * C] = jnp.zeros((16, C), BF16)

    put(1, h1[64:192, :], dp1[64:192, :], acc)

    dh0[...] = dot(dp0[...], proj[0], ((1,), (1,))) * g0[64:256, :]
    acc = [jnp.zeros((8, C), F32) for _ in range(4)]
    for c in range(4, 8):
        delta, qs = back(dh0, (c - 3) * DIL, 0, c, rows(c * DIL), i0[c * DIL:(c + 1) * DIL, :],
                         valid_of[c], gains[0:1, :])
        at = slice((c - 4) * DIL, (c - 3) * DIL)
        out[at, :] = (gr1[at, :] + delta).astype(BF16)
        d = dh0[(c - 3) * DIL:(c - 2) * DIL, :]
        for k in range(3):
            acc[k] += fold8(d * n0[(c - 1 + k) * DIL:(c + k) * DIL, :])
        acc[3] += fold8(qs)
    put(0, h0[96:224, :], dp0[32:160, :], acc)
    keep[...] = act[core]
    send[...] = act[1 - core]


def device(near, far, core):
    z = ((far >> 3) * 2 + (near >> 2) + core) % 8
    x = ((far >> 2) % 2 * 2 + (near >> 1) % 2 + core) % 4
    y = (far % 4 * 2 + near % 2 + core) % 8
    return ((z * 4 + x) * 8 + y) * 2 + core


NEAR = [[device(n, f, c) for n in range(8)] for c in range(2) for f in range(32)]
FAR = [[device(n, (g >> 2) << 3 | x << 2 | g % 4, c) for g in range(16)] for c in range(2) for n in range(8) for x in range(2)]


def own_terms(keep, pick, mine):
    core = lax.axis_index("c")
    q = lax.broadcasted_iota(jnp.int32, (C, 1), 0)
    z = ((((q >> 5) & 1) << 2 | ((q >> 4) & 1) << 1 | ((q >> 8) & 1)) + core) & 7
    x = ((((q >> 3) & 1) << 1 | ((q >> 7) & 1)) + core) & 3
    y = ((((q >> 1) & 3) << 1 | ((q >> 6) & 1)) + core) & 7
    ch = z << 6 | x << 4 | y << 1 | (q & 1)
    pick[...] = (ch == lax.broadcasted_iota(jnp.int32, (C, C), 1)).astype(F32).astype(BF16)
    ha = dot(pick[...], keep[0:128, 0:C], ((1,), (1,))).astype(BF16)
    mine[...] = dot(ha, keep[0:128, C:3 * C], ((1,), (0,)))


def terms(keep, recv, pick, mine, out):
    hb = dot(pick[...], recv[0:128, 0:C], ((1,), (1,))).astype(BF16)
    for j in range(8):
        cols = slice(j * 128, (j + 1) * 128)
        t = mine[:, cols] + dot(hb, recv[0:128, C + j * 128:C + (j + 1) * 128], ((1,), (0,)))
        out[:, j * 64:(j + 1) * 64, :] = t.astype(BF16).reshape(8, 64, 128)
    small = (keep[128:ACT, 0:C].astype(F32) + keep[128:ACT, C:2 * C].astype(F32)
             + recv[128:ACT, 0:C].astype(F32) + recv[128:ACT, C:2 * C].astype(F32))
    tile = jnp.concatenate(
        [small[r:r + 1, 128 * q:128 * (q + 1)] for r in range(4) for q in range(4)], axis=0).astype(BF16)
    for g in range(8):
        out[g, 512:528, :] = tile


def first_sum(recv, out):
    total = recv[0].astype(F32)
    for i in range(1, 8):
        total += recv[i].astype(F32)
    p = lax.broadcasted_iota(jnp.int32, (C, 1), 0)
    src = ((p >> 1) & 7) << 6 | ((p >> 7) & 3) << 4 | ((p >> 4) & 1) << 3 | ((p >> 5) & 3) << 1 | (p & 1)
    pick = (src == lax.broadcasted_iota(jnp.int32, (C, C), 1)).astype(F32).astype(BF16)
    moved = dot(pick, total[0:512, :].astype(BF16), ((1,), (0,)))
    half = jnp.where(lax.axis_index("yl") == 0, total[512:520, :], total[520:528, :])
    for d in range(16):
        out[d] = jnp.concatenate([moved[32 * d:32 * d + 32, :], half], axis=0).astype(BF16)


def second_sum(recv, out):
    total = recv[0].astype(F32)
    for i in range(1, 16):
        total += recv[i].astype(F32)
    swap = (lax.axis_index("c") == 1) & (lax.axis_index("xl") == 0)
    a, b = total[0:16, :], total[16:32, :]
    for i in range(8):
        piece = jnp.where(swap, b, a) if i < 4 else jnp.where(swap, a, b)
        out[i] = jnp.concatenate([piece, total[32:40, :]], axis=0)


def place(recv, proj, taps, gains):
    for c in range(2):
        for y in range(2):
            for j in range(8):
                proj[c, 2 * y:2 * y + 2, j * 128:(j + 1) * 128] = recv[y * 2 + c, 2 * j:2 * j + 2, :] + recv[4 + y * 2 + c, 2 * j:2 * j + 2, :]
        for r in range(4):
            for q in range(4):
                at = 16 + (r % 2) * 4 + q
                row = recv[(r // 2) * 2 + c, at:at + 1, :] + recv[4 + (r // 2) * 2 + c, at:at + 1, :]
                if r < 3:
                    taps[r, c:c + 1, q * 128:(q + 1) * 128] = row
                else:
                    gains[c:c + 1, q * 128:(q + 1) * 128] = row


def call(kernel, ins, outs, scratch=(), mib=48):
    single = not isinstance(outs, (list, tuple))
    vmem = pl.BlockSpec(memory_space=pltpu.VMEM)
    return pl.pallas_call(
        kernel,
        out_shape=outs,
        in_specs=[pl.BlockSpec(memory_space={"v": pltpu.VMEM, "s": pltpu.SMEM, "a": pl.ANY}[m]) for m in ins],
        out_specs=vmem if single else [vmem] * len(outs),
        scratch_shapes=list(scratch),
        compiler_params=pltpu.CompilerParams(vmem_limit_bytes=int(mib * 1024 * 1024)),
    )


def main(*args):
    s = jax.ShapeDtypeStruct
    v = pltpu.VMEM
    return call(
        body,
        "vvvvvvvv",
        [s((128, C), BF16), s((ACT, 3 * C), BF16), s((ACT, 3 * C), BF16)],
        [v((384, C), F32), v((384, 1), F32), v((320, C), F32), v((320, C), BF16), v((320, 2 * C), F32),
         v((320, C), F32), v((320, C), F32), v((320, 1), F32), v((256, C), F32), v((256, C), BF16),
         v((256, 2 * C), F32), v((256, 2 * C), BF16), v((256, C), F32), v((128, C), F32),
         v((192, 2 * C), BF16), v((192, C), F32), v((2, ACT, 3 * C), BF16)],
    )(*args)


def shards(tokens, cotangent, gaps, taps, gains, proj):
    tok, cot = tokens[0], cotangent[0]
    n = 128
    s = jax.ShapeDtypeStruct
    far = [pltpu.with_memory_space_constraint(a, pltpu.HBM) for a in (gaps, tok, cot)]
    down, up = call(pack, "svv", [s((192, C), BF16), s((192, C), BF16)], mib=48)(*far)
    nxt = lax.ppermute(down, SEQ, [(i + 1, i) for i in range(n - 1)])
    prev = lax.ppermute(up, SEQ, [(i, i + 1) for i in range(n - 1)])
    here = [jnp.transpose(taps, (1, 0, 2)), gains, proj]
    here = far + [pltpu.with_memory_space_constraint(a, pltpu.HBM) for a in here]
    near_args = call(
        warm,
        "svvvvv",
        [s((128, 1), F32), s((128, C), BF16), s((128, C), BF16), s((3, 2, C), F32), s((2, C), F32),
         s((2, C, 2 * C), BF16)],
    )(*here)
    tokens_grad, keep, send = main(near_args[0], nxt, prev, *near_args[1:])
    recv = lax.ppermute(send, "c", [(0, 1), (1, 0)])
    pick, mine = call(own_terms, "v", [s((C, C), BF16), s((C, 2 * C), F32)])(keep)
    part = call(terms, "vvvv", s((8, 528, 128), BF16))(keep, recv, pick, mine)
    part = lax.all_to_all(part, ALL, 0, 0, axis_index_groups=NEAR, tiled=True)
    part = call(first_sum, "v", s((16, 40, 128), BF16))(part)
    part = lax.all_to_all(part, ALL, 0, 0, axis_index_groups=FAR, tiled=True)
    part = call(second_sum, "v", s((8, 24, 128), F32))(part)
    part = lax.all_to_all(part, LAST, 0, 0, tiled=True)
    projection_grad, taps_grad, gains_grad = call(
        place, "v", [s((2, 4, 1024), F32), s((3, 2, C), F32), s((2, C), F32)]
    )(part)
    return tokens_grad[None], projection_grad, jnp.transpose(taps_grad, (1, 0, 2)), gains_grad


def solution(mesh):
    fine = Mesh(mesh.devices.reshape(8, 2, 2, 4, 2, 2), ALL)
    return jax.shard_map(
        shards,
        mesh=fine,
        in_specs=(P(HAP, SEQ, None), P(HAP, SEQ, None), P(SEQ, None), P(), P(), P()),
        out_specs=(P(HAP, SEQ, None), P(None, SEQ, None), P(), P()),
        check_vma=False,
    )
```

```python
import jax
import jax.numpy as jnp
from jax import lax
from jax.experimental import pallas as pl
from jax.experimental.pallas import tpu as pltpu
from jax.sharding import Mesh
from jax.sharding import PartitionSpec as P

C = 512
DIL = 32
EPS = 1e-06
F32 = jnp.float32
BF16 = jnp.bfloat16
ALL = ("z", "xh", "xl", "yh", "yl", "c")
LAST = ("xh", "yl", "c")
SEQ = ("z", "xh", "xl", "yh")
HAP = ("yl", "c")
G0 = 0.7978845608028654
G1 = 0.044715
MARK = 64.0
ACT = 144


def gelu_and_slope(x, with_slope=True):
    x2 = x * x
    cdf = 0.5 + 0.5 * jnp.tanh(x * (G0 + (G0 * G1) * x2))
    hid = x * cdf
    if not with_slope:
        return hid, None
    return hid, cdf + hid * (1.0 - cdf) * (2.0 * G0 + (6.0 * G0 * G1) * x2)


def sigmoid(x):
    return 0.5 + 0.5 * jnp.tanh(0.5 * x)


def dot(a, b, dims):
    return lax.dot_general(a, b, (dims, ((), ())), preferred_element_type=F32)


def fold8(v):
    return jnp.sum(v.reshape(v.shape[0] // 8, 8, v.shape[1]), axis=0)


def hi_lo(v):
    hi = v.astype(BF16)
    lo = (v - hi.astype(F32)).astype(BF16)
    return hi, lo


def pack(gaps, tok, cot, up, down):
    at = lax.broadcasted_iota(jnp.int32, (128, 1), 0)
    inside = (at >= gaps[0, 0]) & (at < gaps[0, 1])
    marked = jnp.where(inside, MARK, tok[...].astype(F32)).astype(BF16)
    up[0:128, :] = marked
    down[0:128, :] = marked
    up[128:192, :] = cot[64:128, :]
    down[128:192, :] = cot[0:64, :]


def warm(gaps, tok, cot, taps, gains, proj, valid, tok_out, cot_out, taps_out, gains_out, proj_out):
    at = lax.broadcasted_iota(jnp.int32, (128, 1), 0)
    valid[...] = jnp.where((at >= gaps[0, 0]) & (at < gaps[0, 1]), 0.0, 1.0)
    for a, b in ((tok, tok_out), (cot, cot_out), (taps, taps_out), (gains, gains_out), (proj, proj_out)):
        b[...] = a[...]


def body(own_valid, prev, nxt, tok, cot, taps, gains, proj, out, keep, send,
         n0, i0, g0, h0, ab0, x1, n1, i1, g1, h1, po1, dp1, dh1, gr1, dp0, dh0, act):
    core = lax.axis_index("c")
    place_in_seq = sum(lax.axis_index(a) for a in SEQ)
    inner = (place_in_seq > 0, None, place_in_seq < 12)

    def rows(base):
        ref, at = ((prev, base), (tok, base - 128), (nxt, base - 256))[base // 128]
        return ref[at:at + DIL, :].astype(F32)

    def cot_rows(base):
        if base < 128:
            return prev[128 + base - 64:128 + base - 32, :].astype(F32)
        if base < 256:
            return cot[base - 128:base - 96, :].astype(F32)
        return nxt[128 + base - 256:128 + base - 224, :].astype(F32)

    valid_of = []
    for chunk in range(12):
        if 4 <= chunk < 8:
            valid_of.append(own_valid[DIL * (chunk - 4):DIL * (chunk - 3), :])
        else:
            ref = prev if chunk < 4 else nxt
            lead = ref[DIL * (chunk % 4):DIL * (chunk % 4) + DIL, 0:128].astype(F32)[:, 0:1]
            valid_of.append(jnp.where(lead < 0.5 * MARK, jnp.where(inner[chunk // 4], 1.0, 0.0), 0.0))

    def norm(v, valid, gain):
        inv = lax.rsqrt(jnp.sum(v * v, axis=-1, keepdims=True) * (1.0 / C) + EPS)
        return inv, v * (inv * valid) * gain

    def tap(layer, k):
        return taps[k, layer:layer + 1, :]

    def conv(ref, at, layer):
        return (tap(layer, 0) * ref[at - DIL:at, :] + tap(layer, 1) * ref[at:at + DIL, :]
                + tap(layer, 2) * ref[at + DIL:at + 2 * DIL, :])

    for c in range(12):
        inv, normed = norm(rows(c * DIL), valid_of[c], gains[0:1, :])
        if 4 <= c < 8:
            i0[c * DIL:(c + 1) * DIL, :] = inv
        n0[c * DIL:(c + 1) * DIL, :] = normed
    for c in range(1, 11):
        hid, slope = gelu_and_slope(conv(n0, c * DIL, 0), 3 <= c < 9)
        h0[(c - 1) * DIL:c * DIL, :] = hid.astype(BF16)
        if 3 <= c < 9:
            g0[(c - 1) * DIL:c * DIL, :] = slope
    ab0[...] = dot(h0[...], proj[0], ((1,), (0,)))
    for c in range(1, 11):
        at = slice((c - 1) * DIL, c * DIL)
        first = ab0[at, 0:C]
        gate = sigmoid(ab0[at, C:2 * C])
        both = first * gate
        nx = (rows(c * DIL) + valid_of[c] * both).astype(BF16).astype(F32)
        inv, normed = norm(nx, valid_of[c], gains[1:2, :])
        if 3 <= c < 9:
            ab0[at, 0:C] = gate
            ab0[at, C:2 * C] = both * (1.0 - gate)
            x1[at, :] = nx
            i1[at, :] = inv
        n1[at, :] = normed
    for c in range(2, 10):
        hid, slope = gelu_and_slope(conv(n1, (c - 1) * DIL, 1))
        h1[(c - 2) * DIL:(c - 1) * DIL, :] = hid.astype(BF16)
        g1[(c - 2) * DIL:(c - 1) * DIL, :] = slope
    po1[...] = dot(h1[...], proj[1], ((1,), (0,)))
    for c in range(2, 10):
        at = slice((c - 2) * DIL, (c - 1) * DIL)
        first = po1[at, 0:C]
        gate = sigmoid(po1[at, C:2 * C])
        bg = valid_of[c] * cot_rows(c * DIL) * gate
        dp1[at, 0:C] = bg.astype(BF16)
        dp1[at, C:2 * C] = (bg * first * (1.0 - gate)).astype(BF16)
    dh1[...] = dot(dp1[...], proj[1], ((1,), (1,))) * g1[...]

    def back(dref, c_off, layer, c, sref_rows, inv, valid, gain):
        at = c_off
        dn = (tap(layer, 0) * dref[at + DIL:at + 2 * DIL, :] + tap(layer, 1) * dref[at:at + DIL, :]
              + tap(layer, 2) * dref[at - DIL:at, :])
        dq = dn * valid
        si = sref_rows * inv
        qs = dq * si
        dt = dq * gain
        m = jnp.sum(qs * gain, axis=-1, keepdims=True) * (1.0 / C)
        return inv * (dt - si * m), qs

    def small_rows(parts):
        return [jnp.sum(p, axis=0, keepdims=True) for p in parts]

    acc = [jnp.zeros((8, C), F32) for _ in range(4)]
    for c in range(3, 9):
        at1 = slice((c - 1) * DIL, c * DIL)
        delta, qs = back(dh1, (c - 2) * DIL, 1, c, x1[at1, :], i1[at1, :], valid_of[c], gains[1:2, :])
        grad = cot_rows(c * DIL) + delta
        branch = valid_of[c] * grad
        to = slice((c - 3) * DIL, (c - 2) * DIL)
        dp0[to, 0:C] = (branch * ab0[at1, 0:C]).astype(BF16)
        dp0[to, C:2 * C] = (branch * ab0[at1, C:2 * C]).astype(BF16)
        if 4 <= c < 8:
            gr1[(c - 4) * DIL:(c - 3) * DIL, :] = grad
            d = dh1[(c - 2) * DIL:(c - 1) * DIL, :]
            for k in range(3):
                acc[k] += fold8(d * n1[(c - 2 + k) * DIL:(c - 1 + k) * DIL, :])
            acc[3] += fold8(qs)

    def put(layer, hid, dpr, parts):
        act[layer, 0:128, 0:C] = hid
        act[layer, 0:128, C:3 * C] = dpr
        four = jnp.concatenate(small_rows(parts) + [jnp.zeros((12, C), F32)], axis=0)
        hi, lo = hi_lo(four)
        act[layer, 128:ACT, 0:C] = hi
        act[layer, 128:ACT, C:2 * C] = lo
        act[layer, 128:ACT, 2 * C:3 * C] = jnp.zeros((16, C), BF16)

    put(1, h1[64:192, :], dp1[64:192, :], acc)

    dh0[...] = dot(dp0[...], proj[0], ((1,), (1,))) * g0[64:256, :]
    acc = [jnp.zeros((8, C), F32) for _ in range(4)]
    for c in range(4, 8):
        delta, qs = back(dh0, (c - 3) * DIL, 0, c, rows(c * DIL), i0[c * DIL:(c + 1) * DIL, :],
                         valid_of[c], gains[0:1, :])
        at = slice((c - 4) * DIL, (c - 3) * DIL)
        out[at, :] = (gr1[at, :] + delta).astype(BF16)
        d = dh0[(c - 3) * DIL:(c - 2) * DIL, :]
        for k in range(3):
            acc[k] += fold8(d * n0[(c - 1 + k) * DIL:(c + k) * DIL, :])
        acc[3] += fold8(qs)
    put(0, h0[96:224, :], dp0[32:160, :], acc)
    keep[...] = act[core]
    send[...] = act[1 - core]


def device(near, far, core):
    z = ((far >> 3) * 2 + (near >> 2)) * (1 - 2 * core) % 8
    x = ((far >> 2) % 2 * 2 + (near >> 1) % 2) * (1 - 2 * core) % 4
    y = (far % 4 * 2 + near % 2) * (1 - 2 * core) % 8
    return ((z * 4 + x) * 8 + y) * 2 + core


NEAR = [[device(n, f, c) for n in range(8)] for c in range(2) for f in range(32)]
FAR = [[device(n, (g >> 2) << 3 | x << 2 | g % 4, c) for g in range(16)] for c in range(2) for n in range(8) for x in range(2)]


def own_terms(keep, pick, mine):
    turn = 1 - 2 * lax.axis_index("c")
    q = lax.broadcasted_iota(jnp.int32, (C, 1), 0)
    z = ((((q >> 5) & 1) << 2 | ((q >> 4) & 1) << 1 | ((q >> 8) & 1)) * turn) & 7
    x = ((((q >> 3) & 1) << 1 | ((q >> 7) & 1)) * turn) & 3
    y = ((((q >> 1) & 3) << 1 | ((q >> 6) & 1)) * turn) & 7
    ch = z << 6 | x << 4 | y << 1 | (q & 1)
    pick[...] = (ch == lax.broadcasted_iota(jnp.int32, (C, C), 1)).astype(F32).astype(BF16)
    ha = dot(pick[...], keep[0:128, 0:C], ((1,), (1,))).astype(BF16)
    mine[...] = dot(ha, keep[0:128, C:3 * C], ((1,), (0,)))


def terms(keep, recv, pick, mine, out):
    hb = dot(pick[...], recv[0:128, 0:C], ((1,), (1,))).astype(BF16)
    for j in range(8):
        cols = slice(j * 128, (j + 1) * 128)
        t = mine[:, cols] + dot(hb, recv[0:128, C + j * 128:C + (j + 1) * 128], ((1,), (0,)))
        out[:, j * 64:(j + 1) * 64, :] = t.astype(BF16).reshape(8, 64, 128)
    small = (keep[128:ACT, 0:C].astype(F32) + keep[128:ACT, C:2 * C].astype(F32)
             + recv[128:ACT, 0:C].astype(F32) + recv[128:ACT, C:2 * C].astype(F32))
    tile = jnp.concatenate(
        [small[r:r + 1, 128 * q:128 * (q + 1)] for r in range(4) for q in range(4)], axis=0).astype(BF16)
    for g in range(8):
        out[g, 512:528, :] = tile


def first_sum(recv, out):
    total = recv[0].astype(F32)
    for i in range(1, 8):
        total += recv[i].astype(F32)
    p = lax.broadcasted_iota(jnp.int32, (C, 1), 0)
    src = ((p >> 1) & 7) << 6 | ((p >> 7) & 3) << 4 | ((p >> 4) & 1) << 3 | ((p >> 5) & 3) << 1 | (p & 1)
    pick = (src == lax.broadcasted_iota(jnp.int32, (C, C), 1)).astype(F32).astype(BF16)
    moved = dot(pick, total[0:512, :].astype(BF16), ((1,), (0,)))
    half = jnp.where(lax.axis_index("yl") == 0, total[512:520, :], total[520:528, :])
    for d in range(16):
        out[d] = jnp.concatenate([moved[32 * d:32 * d + 32, :], half], axis=0).astype(BF16)


def second_sum(recv, out):
    total = recv[0].astype(F32)
    for i in range(1, 16):
        total += recv[i].astype(F32)
    swap = (lax.axis_index("c") == 1) & (lax.axis_index("xl") == 1)
    a, b = total[0:16, :], total[16:32, :]
    for i in range(8):
        piece = jnp.where(swap, b, a) if i < 4 else jnp.where(swap, a, b)
        out[i] = jnp.concatenate([piece, total[32:40, :]], axis=0)


def place(recv, proj, taps, gains):
    for c in range(2):
        for y in range(2):
            for j in range(8):
                proj[c, 2 * y:2 * y + 2, j * 128:(j + 1) * 128] = recv[y * 2 + c, 2 * j:2 * j + 2, :] + recv[4 + y * 2 + c, 2 * j:2 * j + 2, :]
        for r in range(4):
            for q in range(4):
                at = 16 + (r % 2) * 4 + q
                row = recv[(r // 2) * 2 + c, at:at + 1, :] + recv[4 + (r // 2) * 2 + c, at:at + 1, :]
                if r < 3:
                    taps[r, c:c + 1, q * 128:(q + 1) * 128] = row
                else:
                    gains[c:c + 1, q * 128:(q + 1) * 128] = row


def call(kernel, ins, outs, scratch=(), mib=48):
    single = not isinstance(outs, (list, tuple))
    vmem = pl.BlockSpec(memory_space=pltpu.VMEM)
    return pl.pallas_call(
        kernel,
        out_shape=outs,
        in_specs=[pl.BlockSpec(memory_space={"v": pltpu.VMEM, "s": pltpu.SMEM, "a": pl.ANY}[m]) for m in ins],
        out_specs=vmem if single else [vmem] * len(outs),
        scratch_shapes=list(scratch),
        compiler_params=pltpu.CompilerParams(vmem_limit_bytes=int(mib * 1024 * 1024)),
    )


def main(*args):
    s = jax.ShapeDtypeStruct
    v = pltpu.VMEM
    return call(
        body,
        "vvvvvvvv",
        [s((128, C), BF16), s((ACT, 3 * C), BF16), s((ACT, 3 * C), BF16)],
        [v((384, C), F32), v((384, 1), F32), v((320, C), F32), v((320, C), BF16), v((320, 2 * C), F32),
         v((320, C), F32), v((320, C), F32), v((320, 1), F32), v((256, C), F32), v((256, C), BF16),
         v((256, 2 * C), F32), v((256, 2 * C), BF16), v((256, C), F32), v((128, C), F32),
         v((192, 2 * C), BF16), v((192, C), F32), v((2, ACT, 3 * C), BF16)],
    )(*args)


def shards(tokens, cotangent, gaps, taps, gains, proj):
    tok, cot = tokens[0], cotangent[0]
    n = 128
    s = jax.ShapeDtypeStruct
    far = [pltpu.with_memory_space_constraint(a, pltpu.HBM) for a in (gaps, tok, cot)]
    up, down = call(pack, "svv", [s((192, C), BF16), s((192, C), BF16)], mib=48)(*far)
    prev = lax.ppermute(up, SEQ, [(i, i + 1) for i in range(n - 1)])
    nxt = lax.ppermute(down, SEQ, [(i + 1, i) for i in range(n - 1)])
    here = [jnp.transpose(taps, (1, 0, 2)), gains, proj]
    here = far + [pltpu.with_memory_space_constraint(a, pltpu.HBM) for a in here]
    near_args = call(
        warm,
        "svvvvv",
        [s((128, 1), F32), s((128, C), BF16), s((128, C), BF16), s((3, 2, C), F32), s((2, C), F32),
         s((2, C, 2 * C), BF16)],
    )(*here)
    tokens_grad, keep, send = main(near_args[0], prev, nxt, *near_args[1:])
    recv = lax.ppermute(send, "c", [(0, 1), (1, 0)])
    pick, mine = call(own_terms, "v", [s((C, C), BF16), s((C, 2 * C), F32)])(keep)
    part = call(terms, "vvvv", s((8, 528, 128), BF16))(keep, recv, pick, mine)
    part = lax.all_to_all(part, ALL, 0, 0, axis_index_groups=NEAR, tiled=True)
    part = call(first_sum, "v", s((16, 40, 128), BF16))(part)
    part = lax.all_to_all(part, ALL, 0, 0, axis_index_groups=FAR, tiled=True)
    part = call(second_sum, "v", s((8, 24, 128), F32))(part)
    part = lax.all_to_all(part, LAST, 0, 0, tiled=True)
    projection_grad, taps_grad, gains_grad = call(
        place, "v", [s((2, 4, 1024), F32), s((3, 2, C), F32), s((2, C), F32)]
    )(part)
    return tokens_grad[None], projection_grad, jnp.transpose(taps_grad, (1, 0, 2)), gains_grad


def solution(mesh):
    fine = Mesh(mesh.devices.reshape(8, 2, 2, 4, 2, 2), ALL)
    return jax.shard_map(
        shards,
        mesh=fine,
        in_specs=(P(HAP, SEQ, None), P(HAP, SEQ, None), P(SEQ, None), P(), P(), P()),
        out_specs=(P(HAP, SEQ, None), P(None, SEQ, None), P(), P()),
        check_vma=False,
    )
```

```python
import jax
import jax.numpy as jnp
from jax import lax
from jax.experimental import pallas as pl
from jax.experimental.pallas import tpu as pltpu
from jax.sharding import Mesh
from jax.sharding import PartitionSpec as P

C = 512
DIL = 32
EPS = 1e-06
F32 = jnp.float32
BF16 = jnp.bfloat16
ALL = ("z", "xh", "xl", "yh", "yl", "c")
LAST = ("xh", "yl", "c")
SEQ = ("z", "xh", "xl", "yh")
HAP = ("yl", "c")
G0 = 0.7978845608028654
G1 = 0.044715
MARK = 64.0
ACT = 144


def gelu_and_slope(x, with_slope=True):
    x2 = x * x
    cdf = 0.5 + 0.5 * jnp.tanh(x * (G0 + (G0 * G1) * x2))
    hid = x * cdf
    if not with_slope:
        return hid, None
    return hid, cdf + hid * (1.0 - cdf) * (2.0 * G0 + (6.0 * G0 * G1) * x2)


def sigmoid(x):
    return 0.5 + 0.5 * jnp.tanh(0.5 * x)


def dot(a, b, dims):
    return lax.dot_general(a, b, (dims, ((), ())), preferred_element_type=F32)


def fold8(v):
    return jnp.sum(v.reshape(v.shape[0] // 8, 8, v.shape[1]), axis=0)


def hi_lo(v):
    hi = v.astype(BF16)
    lo = (v - hi.astype(F32)).astype(BF16)
    return hi, lo


def pack(gaps, tok, cot, down, up):
    at = lax.broadcasted_iota(jnp.int32, (128, 1), 0)
    inside = (at >= gaps[0, 0]) & (at < gaps[0, 1])
    marked = jnp.where(inside, MARK, tok[...].astype(F32)).astype(BF16)
    up[0:128, :] = marked
    down[0:128, :] = marked
    up[128:192, :] = cot[64:128, :]
    down[128:192, :] = cot[0:64, :]


def warm(gaps, tok, cot, taps, gains, proj, valid, tok_out, cot_out, taps_out, gains_out, proj_out):
    at = lax.broadcasted_iota(jnp.int32, (128, 1), 0)
    valid[...] = jnp.where((at >= gaps[0, 0]) & (at < gaps[0, 1]), 0.0, 1.0)
    for a, b in ((tok, tok_out), (cot, cot_out), (taps, taps_out), (gains, gains_out), (proj, proj_out)):
        b[...] = a[...]


def body(own_valid, nxt, prev, tok, cot, taps, gains, proj, out, keep, send,
         n0, i0, g0, h0, ab0, x1, n1, i1, g1, h1, po1, dp1, dh1, gr1, dp0, dh0, act):
    core = lax.axis_index("c")
    place_in_seq = sum(lax.axis_index(a) for a in SEQ)
    inner = (place_in_seq > 0, None, place_in_seq < 12)

    def rows(base):
        ref, at = ((prev, base), (tok, base - 128), (nxt, base - 256))[base // 128]
        return ref[at:at + DIL, :].astype(F32)

    def cot_rows(base):
        if base < 128:
            return prev[128 + base - 64:128 + base - 32, :].astype(F32)
        if base < 256:
            return cot[base - 128:base - 96, :].astype(F32)
        return nxt[128 + base - 256:128 + base - 224, :].astype(F32)

    valid_of = []
    for chunk in range(12):
        if 4 <= chunk < 8:
            valid_of.append(own_valid[DIL * (chunk - 4):DIL * (chunk - 3), :])
        else:
            ref = prev if chunk < 4 else nxt
            lead = ref[DIL * (chunk % 4):DIL * (chunk % 4) + DIL, 0:128].astype(F32)[:, 0:1]
            valid_of.append(jnp.where(lead < 0.5 * MARK, jnp.where(inner[chunk // 4], 1.0, 0.0), 0.0))

    def norm(v, valid, gain):
        inv = lax.rsqrt(jnp.sum(v * v, axis=-1, keepdims=True) * (1.0 / C) + EPS)
        return inv, v * (inv * valid) * gain

    def tap(layer, k):
        return taps[k, layer:layer + 1, :]

    def conv(ref, at, layer):
        return (tap(layer, 0) * ref[at - DIL:at, :] + tap(layer, 1) * ref[at:at + DIL, :]
                + tap(layer, 2) * ref[at + DIL:at + 2 * DIL, :])

    for c in range(12):
        inv, normed = norm(rows(c * DIL), valid_of[c], gains[0:1, :])
        if 4 <= c < 8:
            i0[c * DIL:(c + 1) * DIL, :] = inv
        n0[c * DIL:(c + 1) * DIL, :] = normed
    for c in range(1, 11):
        hid, slope = gelu_and_slope(conv(n0, c * DIL, 0), 3 <= c < 9)
        h0[(c - 1) * DIL:c * DIL, :] = hid.astype(BF16)
        if 3 <= c < 9:
            g0[(c - 1) * DIL:c * DIL, :] = slope
    ab0[...] = dot(h0[...], proj[0], ((1,), (0,)))
    for c in range(1, 11):
        at = slice((c - 1) * DIL, c * DIL)
        first = ab0[at, 0:C]
        gate = sigmoid(ab0[at, C:2 * C])
        both = first * gate
        nx = (rows(c * DIL) + valid_of[c] * both).astype(BF16).astype(F32)
        inv, normed = norm(nx, valid_of[c], gains[1:2, :])
        if 3 <= c < 9:
            ab0[at, 0:C] = gate
            ab0[at, C:2 * C] = both * (1.0 - gate)
            x1[at, :] = nx
            i1[at, :] = inv
        n1[at, :] = normed
    for c in range(2, 10):
        hid, slope = gelu_and_slope(conv(n1, (c - 1) * DIL, 1))
        h1[(c - 2) * DIL:(c - 1) * DIL, :] = hid.astype(BF16)
        g1[(c - 2) * DIL:(c - 1) * DIL, :] = slope
    po1[...] = dot(h1[...], proj[1], ((1,), (0,)))
    for c in range(2, 10):
        at = slice((c - 2) * DIL, (c - 1) * DIL)
        first = po1[at, 0:C]
        gate = sigmoid(po1[at, C:2 * C])
        bg = valid_of[c] * cot_rows(c * DIL) * gate
        dp1[at, 0:C] = bg.astype(BF16)
        dp1[at, C:2 * C] = (bg * first * (1.0 - gate)).astype(BF16)
    dh1[...] = dot(dp1[...], proj[1], ((1,), (1,))) * g1[...]

    def back(dref, c_off, layer, c, sref_rows, inv, valid, gain):
        at = c_off
        dn = (tap(layer, 0) * dref[at + DIL:at + 2 * DIL, :] + tap(layer, 1) * dref[at:at + DIL, :]
              + tap(layer, 2) * dref[at - DIL:at, :])
        dq = dn * valid
        si = sref_rows * inv
        qs = dq * si
        dt = dq * gain
        m = jnp.sum(qs * gain, axis=-1, keepdims=True) * (1.0 / C)
        return inv * (dt - si * m), qs

    def small_rows(parts):
        return [jnp.sum(p, axis=0, keepdims=True) for p in parts]

    acc = [jnp.zeros((8, C), F32) for _ in range(4)]
    for c in range(3, 9):
        at1 = slice((c - 1) * DIL, c * DIL)
        delta, qs = back(dh1, (c - 2) * DIL, 1, c, x1[at1, :], i1[at1, :], valid_of[c], gains[1:2, :])
        grad = cot_rows(c * DIL) + delta
        branch = valid_of[c] * grad
        to = slice((c - 3) * DIL, (c - 2) * DIL)
        dp0[to, 0:C] = (branch * ab0[at1, 0:C]).astype(BF16)
        dp0[to, C:2 * C] = (branch * ab0[at1, C:2 * C]).astype(BF16)
        if 4 <= c < 8:
            gr1[(c - 4) * DIL:(c - 3) * DIL, :] = grad
            d = dh1[(c - 2) * DIL:(c - 1) * DIL, :]
            for k in range(3):
                acc[k] += fold8(d * n1[(c - 2 + k) * DIL:(c - 1 + k) * DIL, :])
            acc[3] += fold8(qs)

    def put(layer, hid, dpr, parts):
        act[layer, 0:128, 0:C] = hid
        act[layer, 0:128, C:3 * C] = dpr
        four = jnp.concatenate(small_rows(parts) + [jnp.zeros((12, C), F32)], axis=0)
        hi, lo = hi_lo(four)
        act[layer, 128:ACT, 0:C] = hi
        act[layer, 128:ACT, C:2 * C] = lo
        act[layer, 128:ACT, 2 * C:3 * C] = jnp.zeros((16, C), BF16)

    put(1, h1[64:192, :], dp1[64:192, :], acc)

    dh0[...] = dot(dp0[...], proj[0], ((1,), (1,))) * g0[64:256, :]
    acc = [jnp.zeros((8, C), F32) for _ in range(4)]
    for c in range(4, 8):
        delta, qs = back(dh0, (c - 3) * DIL, 0, c, rows(c * DIL), i0[c * DIL:(c + 1) * DIL, :],
                         valid_of[c], gains[0:1, :])
        at = slice((c - 4) * DIL, (c - 3) * DIL)
        out[at, :] = (gr1[at, :] + delta).astype(BF16)
        d = dh0[(c - 3) * DIL:(c - 2) * DIL, :]
        for k in range(3):
            acc[k] += fold8(d * n0[(c - 1 + k) * DIL:(c + k) * DIL, :])
        acc[3] += fold8(qs)
    put(0, h0[96:224, :], dp0[32:160, :], acc)
    keep[...] = act[core]
    send[...] = act[1 - core]


def device(near, far, core):
    z = ((far >> 3) * 2 + (near >> 2)) * (1 - 2 * core) % 8
    x = ((far >> 2) % 2 * 2 + (near >> 1) % 2) * (1 - 2 * core) % 4
    y = (far % 4 * 2 + near % 2) * (1 - 2 * core) % 8
    return ((z * 4 + x) * 8 + y) * 2 + core


NEAR = [[device(n, f, c) for n in range(8)] for c in range(2) for f in range(32)]
FAR = [[device(n, (g >> 2) << 3 | x << 2 | g % 4, c) for g in range(16)] for c in range(2) for n in range(8) for x in range(2)]


def own_terms(keep, pick, mine):
    turn = 1 - 2 * lax.axis_index("c")
    q = lax.broadcasted_iota(jnp.int32, (C, 1), 0)
    z = ((((q >> 5) & 1) << 2 | ((q >> 4) & 1) << 1 | ((q >> 8) & 1)) * turn) & 7
    x = ((((q >> 3) & 1) << 1 | ((q >> 7) & 1)) * turn) & 3
    y = ((((q >> 1) & 3) << 1 | ((q >> 6) & 1)) * turn) & 7
    ch = z << 6 | x << 4 | y << 1 | (q & 1)
    pick[...] = (ch == lax.broadcasted_iota(jnp.int32, (C, C), 1)).astype(F32).astype(BF16)
    ha = dot(pick[...], keep[0:128, 0:C], ((1,), (1,))).astype(BF16)
    mine[...] = dot(ha, keep[0:128, C:3 * C], ((1,), (0,)))


def terms(keep, recv, pick, mine, out):
    hb = dot(pick[...], recv[0:128, 0:C], ((1,), (1,))).astype(BF16)
    for j in range(8):
        cols = slice(j * 128, (j + 1) * 128)
        t = mine[:, cols] + dot(hb, recv[0:128, C + j * 128:C + (j + 1) * 128], ((1,), (0,)))
        out[:, j * 64:(j + 1) * 64, :] = t.astype(BF16).reshape(8, 64, 128)
    small = (keep[128:ACT, 0:C].astype(F32) + keep[128:ACT, C:2 * C].astype(F32)
             + recv[128:ACT, 0:C].astype(F32) + recv[128:ACT, C:2 * C].astype(F32))
    tile = jnp.concatenate(
        [small[r:r + 1, 128 * q:128 * (q + 1)] for r in range(4) for q in range(4)], axis=0).astype(BF16)
    for g in range(8):
        out[g, 512:528, :] = tile


def first_sum(recv, out):
    total = recv[0].astype(F32)
    for i in range(1, 8):
        total += recv[i].astype(F32)
    p = lax.broadcasted_iota(jnp.int32, (C, 1), 0)
    src = ((p >> 1) & 7) << 6 | ((p >> 7) & 3) << 4 | ((p >> 4) & 1) << 3 | ((p >> 5) & 3) << 1 | (p & 1)
    pick = (src == lax.broadcasted_iota(jnp.int32, (C, C), 1)).astype(F32).astype(BF16)
    moved = dot(pick, total[0:512, :].astype(BF16), ((1,), (0,)))
    half = jnp.where(lax.axis_index("yl") == 0, total[512:520, :], total[520:528, :])
    for d in range(16):
        out[d] = jnp.concatenate([moved[32 * d:32 * d + 32, :], half], axis=0).astype(BF16)


def second_sum(recv, out):
    total = recv[0].astype(F32)
    for i in range(1, 16):
        total += recv[i].astype(F32)
    swap = (lax.axis_index("c") == 1) & (lax.axis_index("xl") == 1)
    a, b = total[0:16, :], total[16:32, :]
    for i in range(8):
        piece = jnp.where(swap, b, a) if i < 4 else jnp.where(swap, a, b)
        out[i] = jnp.concatenate([piece, total[32:40, :]], axis=0)


def place(recv, proj, taps, gains):
    for c in range(2):
        for y in range(2):
            for j in range(8):
                proj[c, 2 * y:2 * y + 2, j * 128:(j + 1) * 128] = recv[y * 2 + c, 2 * j:2 * j + 2, :] + recv[4 + y * 2 + c, 2 * j:2 * j + 2, :]
        for r in range(4):
            for q in range(4):
                at = 16 + (r % 2) * 4 + q
                row = recv[(r // 2) * 2 + c, at:at + 1, :] + recv[4 + (r // 2) * 2 + c, at:at + 1, :]
                if r < 3:
                    taps[r, c:c + 1, q * 128:(q + 1) * 128] = row
                else:
                    gains[c:c + 1, q * 128:(q + 1) * 128] = row


def call(kernel, ins, outs, scratch=(), mib=48):
    single = not isinstance(outs, (list, tuple))
    vmem = pl.BlockSpec(memory_space=pltpu.VMEM)
    return pl.pallas_call(
        kernel,
        out_shape=outs,
        in_specs=[pl.BlockSpec(memory_space={"v": pltpu.VMEM, "s": pltpu.SMEM, "a": pl.ANY}[m]) for m in ins],
        out_specs=vmem if single else [vmem] * len(outs),
        scratch_shapes=list(scratch),
        compiler_params=pltpu.CompilerParams(vmem_limit_bytes=int(mib * 1024 * 1024)),
    )


def main(*args):
    s = jax.ShapeDtypeStruct
    v = pltpu.VMEM
    return call(
        body,
        "vvvvvvvv",
        [s((128, C), BF16), s((ACT, 3 * C), BF16), s((ACT, 3 * C), BF16)],
        [v((384, C), F32), v((384, 1), F32), v((320, C), F32), v((320, C), BF16), v((320, 2 * C), F32),
         v((320, C), F32), v((320, C), F32), v((320, 1), F32), v((256, C), F32), v((256, C), BF16),
         v((256, 2 * C), F32), v((256, 2 * C), BF16), v((256, C), F32), v((128, C), F32),
         v((192, 2 * C), BF16), v((192, C), F32), v((2, ACT, 3 * C), BF16)],
    )(*args)


def shards(tokens, cotangent, gaps, taps, gains, proj):
    tok, cot = tokens[0], cotangent[0]
    n = 128
    s = jax.ShapeDtypeStruct
    far = [pltpu.with_memory_space_constraint(a, pltpu.HBM) for a in (gaps, tok, cot)]
    down, up = call(pack, "svv", [s((192, C), BF16), s((192, C), BF16)], mib=48)(*far)
    prev = lax.ppermute(up, SEQ, [(i, i + 1) for i in range(n - 1)])
    nxt = lax.ppermute(down, SEQ, [(i + 1, i) for i in range(n - 1)])
    here = [jnp.transpose(taps, (1, 0, 2)), gains, proj]
    here = far + [pltpu.with_memory_space_constraint(a, pltpu.HBM) for a in here]
    near_args = call(
        warm,
        "svvvvv",
        [s((128, 1), F32), s((128, C), BF16), s((128, C), BF16), s((3, 2, C), F32), s((2, C), F32),
         s((2, C, 2 * C), BF16)],
    )(*here)
    tokens_grad, keep, send = main(near_args[0], nxt, prev, *near_args[1:])
    recv = lax.ppermute(send, "c", [(0, 1), (1, 0)])
    pick, mine = call(own_terms, "v", [s((C, C), BF16), s((C, 2 * C), F32)])(keep)
    part = call(terms, "vvvv", s((8, 528, 128), BF16))(keep, recv, pick, mine)
    part = lax.all_to_all(part, ALL, 0, 0, axis_index_groups=NEAR, tiled=True)
    part = call(first_sum, "v", s((16, 40, 128), BF16))(part)
    part = lax.all_to_all(part, ALL, 0, 0, axis_index_groups=FAR, tiled=True)
    part = call(second_sum, "v", s((8, 24, 128), F32))(part)
    part = lax.all_to_all(part, LAST, 0, 0, tiled=True)
    projection_grad, taps_grad, gains_grad = call(
        place, "v", [s((2, 4, 1024), F32), s((3, 2, C), F32), s((2, C), F32)]
    )(part)
    return tokens_grad[None], projection_grad, jnp.transpose(taps_grad, (1, 0, 2)), gains_grad


def solution(mesh):
    fine = Mesh(mesh.devices.reshape(8, 2, 2, 4, 2, 2), ALL)
    return jax.shard_map(
        shards,
        mesh=fine,
        in_specs=(P(HAP, SEQ, None), P(HAP, SEQ, None), P(SEQ, None), P(), P(), P()),
        out_specs=(P(HAP, SEQ, None), P(None, SEQ, None), P(), P()),
        check_vma=False,
    )
```
